1024 devices in a mesh: slab: 64 (over x_lo, z), blk: 16 (over x_hi, y, core).
Axes of the slice: x: 4 (x_hi: 2, x_lo: 2; x = x_hi * 2 + x_lo), y: 4, z: 32, core: 2. Of those that a mesh axis runs over, the one named last changes fastest.
Arguments:
- density: float32 [256, 256, 128], P('slab', 'blk'), may hold values from 0.05 to 1
- solid: int32 [256, 256, 128], P('slab', 'blk'), may hold values 0 or 1
- load: float32 [3, 256, 256, 128], P(None, 'slab', 'blk'), may hold values from -6 to 6
- start: float32 [3, 256, 256, 128], P(None, 'slab', 'blk'), may hold values from -4.5 to 7
- stencil: float32 [27, 3, 3], replicated, as said below
- owner: int32 [64, 16, 64, 1], P('slab', 'blk'), may hold values from 0 to 15; in each aligned block of 64 rows (0 to 63, 64 to 127, ..., all dimensions but the last counted through in order) at most 10 rows name the same one
Outputs:
- displacement: float32 [3, 256, 256, 128], P(None, 'slab', 'blk')
- owned: float32 [64, 16, 16, 10, 128], P('slab', 'blk')
The draws below stay inside these ranges and needn't reach their ends.
Inputs may be any that keep to these rules, and one draw needn't show every extreme that they name: Among the 64 blocks of one device no owner is named more than 10 times, a bound that some block reaches. For every row a of every offset block the stencil's center entry stencil[13, a, a] exceeds the sum of the magnitudes of all other entries of row a over all offsets.
All inputs are finite; a program needn't handle non-finite values. No bound on the sum of `solid` on one device may be relied on, other than what follows from the above.
Results may differ from the reference program's by a relative error of at most 0.0001.
Values sent between devices are 32-bit elements; how exact they have to be, the bound alone decides.
A program may use at most 32 MiB of HBM per device.

```python
import math
import jax
import jax.numpy as jnp
import numpy as np
from jax import lax

CX = 4
CY = 16
CZ = 128
BLOCK = 128
NX = 256
NY = 256
BLOCKS_DEV = 64
CAP = 10
N_SLAB = 64
N_BLK = 16


TWO_PI = 6.283185307179586


def draw_stencil(key, part):
    key_off = jax.random.fold_in(key, 11)
    key_diag = jax.random.fold_in(key, 12)
    key_cross = jax.random.fold_in(key, 13)
    key_mag = jax.random.fold_in(key, 14)
    eye_mat = jnp.eye(3, dtype=jnp.float32)
    magnitude = jax.random.uniform(key_mag, (27, 3), jnp.float32, 0.0, 1.0)
    diag_mag = 0.06 + 0.03 * magnitude
    cross = jax.random.uniform(key_off, (27, 3, 3), jnp.float32, -1.0, 1.0) * 0.004
    offdiag = cross * (1.0 - eye_mat)[None] - diag_mag[:, :, None] * eye_mat[None]
    diag_vals = 2.8 + jax.random.uniform(key_diag, (3,), jnp.float32, 0.0, 0.4)
    center = jax.random.uniform(key_cross, (3, 3), jnp.float32, -0.1, 0.1) * (1.0 - eye_mat) + diag_vals[:, None] * eye_mat
    return offdiag.at[13].set(center).astype(jnp.float32)


def draw_start(key, part):
    key_mean = jax.random.fold_in(key, 21)
    key_rough = jax.random.fold_in(key, 22)
    key_phase = jax.random.fold_in(key, 23)
    means = jax.random.uniform(key_mean, (3,), jnp.float32, 1.2, 2.0)
    phase = jax.random.uniform(key_phase, (3,), jnp.float32, 0.0, TWO_PI)
    places = jnp.arange(NX, dtype=jnp.float32) / NX
    smooth = means[:, None] * (1.0 + 0.25 * jnp.cos(TWO_PI * places[None, :] + phase[:, None]))
    rough = jnp.clip(jax.random.normal(key_rough, (3, NX, NY, CZ), jnp.float32), -4.0, 4.0)
    return (smooth[:, :, None, None] + rough).astype(jnp.float32)


def with_ends(array, key, smallest, high):
    longest = array.shape.index(max(array.shape))
    spots = []
    for shift in (0, 1):
        where = [jax.random.randint(jax.random.fold_in(key, axis), (), 0, length) for axis, length in enumerate(array.shape)]
        where[longest] = (where[longest] + shift) % array.shape[longest]
        spots.append(tuple(where))
    return array.at[spots[0]].set(smallest).at[spots[1]].set(high)


def block_levels(rng, extent, shards, least, top_value):
    def one(dim, blocks):
        draws = jax.random.uniform(jax.random.fold_in(jax.random.fold_in(rng, 6), dim), (blocks,), jnp.float32, least / len(shards), top_value / len(shards))
        return jnp.repeat(jnp.exp(draws), extent[dim] // blocks).reshape((-1,) + (1,) * (len(extent) - dim - 1))

    level = one(*shards[0])
    for cut in shards[1:]:
        level = level * one(*cut)
    return level


def shared_out(key, own, number, rows, count, top, most, slope):
    sequence = jax.random.permutation(key, count)
    heavy_load, usual = load_shares(count, rows * top, most, slope, True), load_shares(count, rows * top, most, slope, False)
    places = jnp.arange(count)

    def named(tallies, offset_by):
        used = int((tallies > 0).sum())
        fixed = max(1, used // 4)
        passed = fixed + (places - fixed + offset_by * (used - fixed)) % max(1, count - fixed)
        return jnp.zeros((count,), jnp.int32).at[sequence[jnp.where(places < fixed, places, passed)]].set(jnp.asarray(tallies, jnp.int32))

    tallies = jnp.where(number % 4 == 0, named(heavy_load, number // 4), named(usual, number - number // 4 - 1))
    mixed = jax.random.permutation(jax.random.fold_in(own, 3), count)
    source_of, sink = mixed[0:count // 2 * 2:2], mixed[1:count // 2 * 2:2]
    slack = jnp.minimum(tallies[source_of] - 1, most - tallies[sink]) // 2
    slack = jnp.where((source_of == sequence[0]) | (sink == sequence[0]) | (tallies[sink] == 0), 0, jnp.maximum(slack, 0))
    passed = jax.random.randint(jax.random.fold_in(own, 4), (count // 2,), 0, 1 << 20) % (slack + 1)
    tallies = tallies.at[source_of].add(-passed).at[sink].add(passed)
    members = jnp.searchsorted(jnp.cumsum(tallies), jnp.arange(rows * top), side="right").astype(jnp.int32)
    listing = members.reshape(top, rows).T
    listing = listing[jax.random.permutation(jax.random.fold_in(own, 1), rows)]
    offset_by = jax.random.randint(jax.random.fold_in(own, 2), (rows, 1), 0, top)
    return jnp.take_along_axis(listing, (jnp.arange(top)[None, :] + offset_by) % top, axis=1)


def load_shares(number_of, total, most, lean, full):
    loads = [(1 << 20) // math.isqrt(grade ** lean) + 1 for grade in range(1, number_of + 1)]
    largest = most if full else min(most, max(-(-total // number_of), total * loads[0] // sum(loads)))
    least = 1 if total - largest >= number_of - 1 else 0
    given, surplus = [largest] + [least] * (number_of - 1), total - largest - least * (number_of - 1)
    while surplus > 0:
        movable = [i for i in range(1, number_of) if given[i] < largest] or [i for i in range(1, number_of) if given[i] < most]
        pool, remaining = sum([loads[i] for i in movable]), surplus
        for i in movable:
            more = min(most - given[i], max(1, remaining * loads[i] // pool), surplus)
            given[i] = given[i] + more
            surplus = surplus - more
    return np.array(given)


def gaussian(rng, shape, width, most, cuts=(), kind=jnp.bfloat16):
    level = block_levels(rng, shape, cuts, -0.22, 0.18) if cuts else 1.0
    array = jax.random.normal(rng, shape, jnp.float32) * width * level
    return jnp.minimum(jnp.maximum(array, -most), most).astype(kind)


def setup_inputs(seed: int = 0) -> dict:
    seeds = jax.random.split(jax.random.key(seed), 7)
    density = jnp.clip(0.05 + 0.95 * jax.random.uniform(seeds[0], (NX, NY, CZ), jnp.float32) ** block_levels(seeds[0], (NX, NY, CZ), ((0, 64), (1, 16)), -0.2, 0.2), 0.05, 1.0)
    solid = with_ends((jax.random.randint(seeds[1], (NX, NY, CZ), 0, 4) < 3).astype(jnp.int32), jax.random.fold_in(seeds[1], 1), 0, 1)
    load = gaussian(seeds[2], (3, NX, NY, CZ), 1.0, 6.0, ((1, 64), (2, 16)), jnp.float32)
    start = draw_start(jax.random.fold_in(seeds[6], 71), 0)
    stencil = draw_stencil(jax.random.fold_in(seeds[6], 71), 0)
    owner_keys = jax.random.split(jax.random.fold_in(seeds[5], 1), N_SLAB * N_BLK * BLOCKS_DEV // BLOCKS_DEV)
    owner_turns = jax.random.permutation(jax.random.fold_in(seeds[5], 3), N_SLAB * N_BLK * BLOCKS_DEV // BLOCKS_DEV)
    owner = jax.vmap(lambda own, number: shared_out(jax.random.fold_in(seeds[5], 2), own, number, BLOCKS_DEV, N_BLK, 1, CAP, 2))(owner_keys, owner_turns).reshape((N_SLAB, N_BLK, BLOCKS_DEV, 1))
    return dict(density=density, solid=solid, load=load, start=start, stencil=stencil, owner=owner)


WEIGHTS = (1.0, 2.0, 3.0, 4.0, 5.0, 4.0, 3.0, 2.0, 1.0)
OMEGA = 0.6
EMIN = 0.1
PENAL = 3.0


def smooth_axis(padded, axis, count):
    result = WEIGHTS[0] * lax.slice_in_dim(padded, 0, count, axis=axis)
    for shift in range(1, 9):
        result = result + WEIGHTS[shift] * lax.slice_in_dim(padded, shift, shift + count, axis=axis)
    return result


def design_filter(field):
    rows, cols, depth = field.shape
    padded = jnp.pad(field, 4)
    padded = smooth_axis(padded, 0, rows)
    padded = smooth_axis(padded, 1, cols)
    return smooth_axis(padded, 2, depth)


def stencil_sum(padded, stencil):
    rows = padded.shape[1] - 2
    cols = padded.shape[2] - 2
    depth = padded.shape[3] - 2
    result = None
    for step_x in range(3):
        views = []
        for step_y in range(3):
            for step_z in range(3):
                views.append(padded[:, step_x:step_x + rows, step_y:step_y + cols, step_z:step_z + depth])
        stacked = jnp.stack(views).reshape(27, rows * cols * depth)
        coeffs = stencil[9 * step_x:9 * step_x + 9].transpose(1, 0, 2).reshape(3, 27)
        contrib = jnp.dot(coeffs, stacked, precision=lax.Precision.HIGHEST, preferred_element_type=jnp.float32)
        result = contrib if result is None else result + contrib
    return result.reshape(3, rows, cols, depth)


def apply_operator(field, stencil):
    return stencil_sum(jnp.pad(field, ((0, 0), (1, 1), (1, 1), (1, 1))), stencil)


def restrict(field):
    lead = field.shape[0]
    rows, cols, depth = field.shape[1:]
    shaped = field.reshape(lead, rows // 2, 2, cols // 2, 2, depth // 2, 2)
    return jnp.mean(shaped, axis=(2, 4, 6))


def prolong(field):
    field = jnp.repeat(field, 2, axis=1)
    field = jnp.repeat(field, 2, axis=2)
    return jnp.repeat(field, 2, axis=3)


def deliver(filtered, owner):
    slabs, groups, per_dev = owner.shape[0], owner.shape[1], owner.shape[2]
    depth = filtered.shape[2]
    blocks = filtered.reshape(slabs, CX, groups, CY, depth).transpose(0, 2, 1, 3, 4).reshape(slabs, groups, per_dev, BLOCK)
    names = owner[..., 0]
    onehot = (names[..., None] == jnp.arange(groups, dtype=jnp.int32)).astype(jnp.int32)
    rank = jnp.sum((jnp.cumsum(onehot, axis=2) - 1) * onehot, axis=-1)
    slab_idx = jnp.arange(slabs, dtype=jnp.int32)[:, None, None]
    src_idx = jnp.arange(groups, dtype=jnp.int32)[None, :, None]
    owned = jnp.zeros((slabs, groups, groups, CAP, BLOCK), jnp.float32)
    return owned.at[slab_idx, names, src_idx, rank].set(blocks)


def reference(density, solid, load, start, stencil, owner):
    weight_sum = design_filter(jnp.ones_like(density))
    xphys = design_filter(density) / weight_sum
    solid_field = solid.astype(jnp.float32)
    young = EMIN + solid_field * (xphys * xphys * xphys)
    center_diag = jnp.diagonal(stencil[13])[:, None, None, None]
    scale = young[None] * center_diag
    first = start + OMEGA * (load - young[None] * apply_operator(start, stencil)) / scale
    resid = load - young[None] * apply_operator(first, stencil)
    coarse_resid = restrict(resid)
    coarse_young = restrict(young[None])[0]
    coarse_scale = coarse_young[None] * center_diag
    corr_one = OMEGA * coarse_resid / coarse_scale
    corr_two = corr_one + OMEGA * (coarse_resid - coarse_young[None] * apply_operator(corr_one, stencil)) / coarse_scale
    displacement = first + prolong(corr_two)
    energy = jnp.sum(displacement * apply_operator(displacement, stencil), axis=0)
    sens = -PENAL * xphys * xphys * solid_field * energy
    filtered = design_filter(density * sens) / (weight_sum * density)
    return displacement, deliver(filtered, owner)
```

```python
import functools

import jax
import jax.numpy as jnp
from jax import lax
from jax.experimental import pallas as pl
from jax.experimental.pallas import tpu as pltpu
from jax.sharding import PartitionSpec as P

OMEGA = 0.6
EMIN = 0.1
CAP = 10
MESH = pl.DeviceIdType.MESH
F32 = jnp.float32
BF16 = jnp.bfloat16
DIRS = ((1, 0), (-1, 0), (0, 1), (0, -1), (1, 1), (1, -1), (-1, 1), (-1, -1))


def iota(shape, dim):
    return lax.broadcasted_iota(jnp.int32, shape, dim)


def split2(value):
    high = value.astype(BF16).astype(F32)
    return high, value - high


def split3(value):
    high, rest = split2(value)
    mid, low = split2(rest)
    return high, mid, low


def lane_mod(lanes, size, count):
    for step in range(count, 0, -1):
        lanes = jnp.where(lanes >= size * step, lanes - size * step, lanes)
    return lanes


def band_position(window, wide, has_low, has_high):
    far = jnp.int32(-1000)
    low_off = jnp.where(has_low, jnp.int32(-16 - wide), far)
    high_off = jnp.where(has_high, jnp.int32(-wide), far)
    outside = jnp.where(window < 16 + wide, window + low_off, window + high_off)
    outside = jnp.where(window >= 16 + 2 * wide, far, outside)
    return jnp.where(window < 16, window, outside)


def band_matrix(st_ref, ex, rows_y, rows, wide, dilate, flags, scale, centre):
    lanes = iota((rows, 216), 1)
    window = lane_mod(lanes, 24, 8)
    position = band_position(window, wide, *flags)
    target = rows_y(iota((rows, 216), 0))
    masks = [position == target + dilate * (ey - 1) for ey in range(3)]
    lane_row = iota((1, 216), 1)
    in_comp = lane_mod(lane_row, 72, 2)
    first_comp, second_comp = in_comp < 24, in_comp < 48
    use_high = lanes < 144
    blocks = []
    for ez in range(3):
        for a in range(3):
            total = jnp.zeros((rows, 216), F32)
            for ey in range(3):
                off = 9 * ex + 3 * ey + ez
                coef = jnp.where(
                    first_comp,
                    st_ref[a, 0, off],
                    jnp.where(second_comp, st_ref[a, 1, off], st_ref[a, 2, off]),
                )
                if scale is not None:
                    coef = coef * scale[a]
                    if off == 13:
                        own = (in_comp >= 24 * a) & (in_comp < 24 * a + 24)
                        coef = coef + jnp.where(own, F32(centre), F32(0.0))
                total = jnp.where(masks[ey], coef, total)
            high, low = split2(total)
            blocks.append(jnp.where(use_high, high, low))
    return jnp.concatenate(blocks, axis=0).astype(BF16)


def stencil_apply(planes, mat_ref, rows, dilate):
    parts = []
    for plane in planes:
        high, low = split2(plane)
        parts.append(jnp.concatenate([high, low, high], axis=0).astype(BF16))
    total = None
    for ex in range(3):
        right = jnp.concatenate(parts[ex : ex + 4], axis=1)
        piece = jnp.dot(mat_ref[ex], right, preferred_element_type=F32)
        total = piece if total is None else total + piece
    size = 3 * rows
    lanes = iota((size, 128), 1)
    result = []
    for x in range(4):
        down, mid, up = (
            total[ez * size : (ez + 1) * size, x * 128 : (x + 1) * 128] for ez in range(3)
        )
        down = jnp.where(lanes >= dilate, pltpu.roll(down, dilate, 1), 0.0)
        up = jnp.where(lanes < 128 - dilate, pltpu.roll(up, 128 - dilate, 1), 0.0)
        result.append(mid + down + up)
    return result


def smooth(win_ref, wy_ref, wz_ref, mask_low, mask_high):
    planes = [win_ref[i] for i in range(12)]
    planes = [
        v * mask_low if i < 4 else v * mask_high if i >= 8 else v for i, v in enumerate(planes)
    ]
    sums = []
    for x in range(4):
        v = planes[x : x + 9]
        sums.append(
            (v[0] + v[8])
            + 2.0 * (v[1] + v[7])
            + 3.0 * (v[2] + v[6])
            + 4.0 * (v[3] + v[5])
            + 5.0 * v[4]
        )
    stacked = jnp.concatenate(split3(jnp.concatenate(sums, axis=1)), axis=0).astype(BF16)
    cols = jnp.dot(wy_ref[...], stacked, preferred_element_type=F32)
    cols = jnp.concatenate([cols[:, x * 128 : (x + 1) * 128] for x in range(4)], axis=0)
    pair = jnp.concatenate(split2(cols), axis=1).astype(BF16)
    return jnp.dot(pair, wz_ref[...], preferred_element_type=F32)


def edge_weight(place, extent):
    def missing(n):
        n = jnp.maximum(n, 0)
        return lax.shift_right_logical(n * (n + 1), 1)

    return (25 - missing(4 - place) - missing(5 + place - extent)).astype(F32)


def pair_sum(value, axis, size):
    index = iota(value.shape, axis)
    even = lax.rem(index, 2) == 0
    return value + jnp.where(
        even, pltpu.roll(value, size - 1, axis), pltpu.roll(value, 1, axis)
    )


def kernel(
    slabs,
    groups,
    cap,
    density,
    solid,
    load,
    start,
    st_ref,
    owner,
    disp_ref,
    owned_ref,
    dens_win,
    sens_win,
    f0,
    f1,
    coarse,
    load_v,
    solid_v,
    packed,
    mat1,
    mat2,
    wy_ref,
    wz_ref,
    pick_ref,
    local_sem,
    send_sem,
    recv_sem,
    give_sem,
    take_sem,
):
    p = lax.axis_index("slab")
    s = lax.axis_index("blk")

    def neighbour(dx, dy):
        return (lax.rem(p + dx + slabs, slabs), lax.rem(s + dy + groups, groups))

    locals_ = [
        pltpu.make_async_copy(start, f0.at[:, 1:5, 0:16], local_sem.at[0]),
        pltpu.make_async_copy(density, dens_win.at[4:8, 0:16], local_sem.at[1]),
        pltpu.make_async_copy(load, load_v, local_sem.at[2]),
        pltpu.make_async_copy(solid, solid_v, local_sem.at[3]),
    ]
    f0[:, :, 16:24] = jnp.zeros((3, 6, 8, 128), F32)
    f1[:, :, 16:24] = jnp.zeros((3, 6, 8, 128), F32)
    for copy in locals_:
        copy.start()

    barrier = pltpu.get_barrier_semaphore()
    partners = [neighbour(dx, dy) for dx, dy in DIRS if dx != 0]
    partners += [(p, lax.rem(s + d, groups)) for d in range(1, groups)]
    for partner in partners:
        pl.semaphore_signal(barrier, inc=1, device_id=partner, device_id_type=MESH)
    pl.semaphore_wait(barrier, len(partners))

    def remote(src, dst, row, i):
        return pltpu.make_async_remote_copy(
            src_ref=src,
            dst_ref=dst,
            send_sem=send_sem.at[row, i],
            recv_sem=recv_sem.at[row, i],
            device_id=neighbour(*DIRS[i]),
            device_id_type=MESH,
        )

    started = []

    def exchange(row, make):
        copies = [remote(*make(dx, dy), row, i) for i, (dx, dy) in enumerate(DIRS)]
        for copy in copies:
            copy.start()
        started.extend(copies)
        return copies

    def field_slices(src, base, dst):
        def make(dx, dy):
            sx = (base + 3, base, slice(base, base + 4))[(dx == -1) + 2 * (dx == 0)]
            tx = (0, 5, slice(1, 5))[(dx == -1) + 2 * (dx == 0)]
            sy = ((15, 16), (0, 1), (0, 16))[(dy == -1) + 2 * (dy == 0)]
            ty = ((16, 17), (17, 18), (0, 16))[(dy == -1) + 2 * (dy == 0)]
            return src.at[:, sx, sy[0] : sy[1]], dst.at[:, tx, ty[0] : ty[1]]

        return make

    def wide_slices(src, base, dst):
        def make(dx, dy):
            tx = (0, 8, 4)[(dx == -1) + 2 * (dx == 0)]
            sy = ((12, 16), (0, 4), (0, 16))[(dy == -1) + 2 * (dy == 0)]
            ty = ((16, 20), (20, 24), (0, 16))[(dy == -1) + 2 * (dy == 0)]
            return (
                src.at[base : base + 4, sy[0] : sy[1]],
                dst.at[tx : tx + 4, ty[0] : ty[1]],
            )

        return make

    def coarse_slices(dx, dy):
        tx = (0, 2, 1)[(dx == -1) + 2 * (dx == 0)]
        sy = ((12, 16), (0, 4), (0, 16))[(dy == -1) + 2 * (dy == 0)]
        ty = ((16, 20), (20, 24), (0, 16))[(dy == -1) + 2 * (dy == 0)]
        return coarse.at[:, 1, sy[0] : sy[1]], coarse.at[:, tx, ty[0] : ty[1]]

    start_in = exchange(0, field_slices(start, 0, f0))
    dens_in = exchange(1, wide_slices(density, 0, dens_win))

    flags = (s > 0, s < groups - 1)
    mask_low = jnp.where(p > 0, 1.0, 0.0).astype(F32)
    mask_high = jnp.where(p < slabs - 1, 1.0, 0.0).astype(F32)
    for ex in range(3):
        mat1[ex] = band_matrix(st_ref, ex, lambda r: r, 16, 1, 1, flags, None, 0.0)
    wy_pos = band_position(lane_mod(iota((16, 72), 1), 24, 2), 4, *flags)
    wy_ref[...] = jnp.maximum(5 - jnp.abs(wy_pos - iota((16, 72), 0)), 0).astype(F32).astype(BF16)
    wz_row = lane_mod(iota((256, 128), 0), 128, 1)
    wz_ref[...] = (
        jnp.maximum(5 - jnp.abs(wz_row - iota((256, 128), 1)), 0).astype(F32).astype(BF16)
    )
    weight_y = edge_weight(s * 16 + iota((16, 128), 0), 16 * groups)
    weight_z = edge_weight(iota((16, 128), 1), 128)
    weight_yz = weight_y * weight_z
    weight = jnp.concatenate(
        [
            weight_yz * edge_weight(jnp.full((16, 128), p * 4 + x, jnp.int32), 4 * slabs)
            for x in range(4)
        ],
        axis=0,
    )
    inv_weight = 1.0 / weight
    relax = [OMEGA / jnp.full((8, 128), st_ref[a, a, 13], F32)[0:1, :] for a in range(3)]

    names = owner[...].astype(F32)
    down, across = iota((64, 64), 0), iota((64, 64), 1)
    names_col = jnp.sum(jnp.where(down == across, names, 0.0), axis=1, keepdims=True)
    earlier = (names_col == names) & (across < down)
    rank = jnp.sum(jnp.where(earlier, 1.0, 0.0), axis=1, keepdims=True)
    code_col = names_col * 16.0 + rank
    spread = iota((64, 192), 0) == lane_mod(iota((64, 192), 1), 64, 2)
    code_row = jnp.sum(jnp.where(spread, code_col, 0.0), axis=0, keepdims=True)
    slot = iota((16 * groups, 192), 0).astype(F32)
    pick_ref[...] = jnp.where(slot == code_row, 1.0, 0.0).astype(BF16)

    def field_planes(ref):
        planes = [ref[:, j].reshape(72, 128) for j in range(6)]
        planes[0] = planes[0] * mask_low
        planes[5] = planes[5] * mask_high
        return planes

    locals_[0].wait()
    for copy in start_in:
        copy.wait_recv()
    s_start = stencil_apply(field_planes(f0), mat1, 16, 1)
    locals_[1].wait()
    locals_[2].wait()
    locals_[3].wait()
    for copy in dens_in:
        copy.wait_recv()
    xphys = smooth(dens_win, wy_ref, wz_ref, mask_low, mask_high) * inv_weight
    solid_f = solid_v[...].astype(F32).reshape(64, 128)
    young = EMIN + solid_f * (xphys * xphys * xphys)
    inv_young = 1.0 / young
    for a in range(3):
        for x in range(4):
            rows = slice(16 * x, 16 * x + 16)
            f1[a, 1 + x, 0:16] = f0[a, 1 + x, 0:16] + relax[a] * (
                load_v[a, x] * inv_young[rows] - s_start[x][16 * a : 16 * a + 16]
            )
    first_in = exchange(2, field_slices(f1, 1, f1))

    dens = dens_win[4:8, 0:16].reshape(64, 128)
    sens_scale = (-3.0 * dens) * (xphys * xphys) * solid_f
    out_scale = inv_weight / dens
    lanes16 = iota((16, 128), 1)
    even_lane = lax.rem(lanes16, 2) == 0

    def coarsen(quarter):
        halves = [
            pair_sum(pair_sum(quarter[2 * i] + quarter[2 * i + 1], 1, 128), 0, 16) * 0.125
            for i in range(2)
        ]
        return jnp.where(even_lane, halves[0], halves[1])

    coarse[3, 1, 0:16] = coarsen([young[16 * x : 16 * x + 16] for x in range(4)])

    def coarse_y(r):
        return jnp.where(r < 16, r, jnp.where(r == 16, -1, jnp.where(r == 17, 16, -5000)))

    for ex in range(3):
        tall = [-relax[a][:, 0:1] for a in range(3)]
        mat2[ex] = band_matrix(st_ref, ex, coarse_y, 24, 4, 2, flags, tall, 2.0)

    for copy in first_in:
        copy.wait_recv()
    s_first = stencil_apply(field_planes(f1), mat1, 16, 1)
    for a in range(3):
        coarse[a, 1, 0:16] = coarsen(
            [
                load_v[a, x] - young[16 * x : 16 * x + 16] * s_first[x][16 * a : 16 * a + 16]
                for x in range(4)
            ]
        )
    coarse_in = exchange(3, coarse_slices)
    for copy in coarse_in:
        copy.wait_recv()

    lanes72 = iota((24, 128), 1)
    even72 = lax.rem(lanes72, 2) == 0
    corr_planes = []
    for plane in range(3):
        inv_cy = 1.0 / coarse[3, plane]
        both = [relax[a] * (coarse[a, plane] * inv_cy) for a in range(3)]
        if plane == 0:
            both = [v * mask_low for v in both]
        if plane == 2:
            both = [v * mask_high for v in both]
        lower = [jnp.where(even72, v, pltpu.roll(v, 1, 1)) for v in both]
        upper = [jnp.where(even72, pltpu.roll(v, 127, 1), v) for v in both]
        corr_planes.append(jnp.concatenate(lower, axis=0))
        corr_planes.append(jnp.concatenate(upper, axis=0))
    corr = stencil_apply(corr_planes, mat2, 24, 2)

    disp = []
    for j, c in enumerate((0, 1, 1, 2, 2, 3)):
        disp.append(f1[:, j].reshape(72, 128) + corr[c])
    masked = [disp[0] * mask_low, *disp[1:5], disp[5] * mask_high]
    s_disp = stencil_apply(masked, mat1, 16, 1)
    for x in range(4):
        energy = None
        for a in range(3):
            term = disp[1 + x][24 * a : 24 * a + 16] * s_disp[x][16 * a : 16 * a + 16]
            energy = term if energy is None else energy + term
        sens_win[4 + x, 0:16] = sens_scale[16 * x : 16 * x + 16] * energy
    sens_in = exchange(4, wide_slices(sens_win, 4, sens_win))
    for x in range(4):
        for a in range(3):
            disp_ref[a, x] = disp[1 + x][24 * a : 24 * a + 16]
    for copy in sens_in:
        copy.wait_recv()
    filtered = smooth(sens_win, wy_ref, wz_ref, mask_low, mask_high) * out_scale

    three = jnp.concatenate(split3(filtered), axis=0).astype(BF16)
    rows = jnp.dot(pick_ref[...], three, preferred_element_type=F32)
    for j in range(groups):
        packed[j] = rows[16 * j : 16 * j + cap]
    gives = []
    for d in range(1, groups):
        target = lax.rem(s + d, groups)
        gives.append(
            pltpu.make_async_remote_copy(
                src_ref=packed.at[target],
                dst_ref=owned_ref.at[s],
                send_sem=give_sem.at[d],
                recv_sem=take_sem.at[d],
                device_id=(p, target),
                device_id_type=MESH,
            )
        )
        gives[-1].start()
    owned_ref[s] = packed[s]
    for copy in gives:
        copy.wait_recv()
    for copy in started + gives:
        copy.wait_send()


def on_device(density, solid, load, start, stencil, owner):
    slabs, groups = lax.axis_size("slab"), lax.axis_size("blk")
    cap = CAP
    hbm = pl.BlockSpec(memory_space=pltpu.HBM)
    vmem = pl.BlockSpec(memory_space=pltpu.VMEM)
    disp, owned = pl.pallas_call(
        functools.partial(kernel, slabs, groups, cap),
        out_shape=(
            jax.ShapeDtypeStruct(load.shape, F32),
            jax.ShapeDtypeStruct((groups, cap, 128), F32),
        ),
        in_specs=[hbm, hbm, hbm, hbm, pl.BlockSpec(memory_space=pltpu.SMEM), vmem],
        out_specs=(vmem, vmem),
        scratch_shapes=[
            pltpu.VMEM((12, 24, 128), F32),
            pltpu.VMEM((12, 24, 128), F32),
            pltpu.VMEM((3, 6, 24, 128), F32),
            pltpu.VMEM((3, 6, 24, 128), F32),
            pltpu.VMEM((4, 3, 24, 128), F32),
            pltpu.VMEM((3, 4, 16, 128), F32),
            pltpu.VMEM((4, 16, 128), jnp.int32),
            pltpu.VMEM((groups, cap, 128), F32),
            pltpu.VMEM((3, 144, 216), BF16),
            pltpu.VMEM((3, 216, 216), BF16),
            pltpu.VMEM((16, 72), BF16),
            pltpu.VMEM((256, 128), BF16),
            pltpu.VMEM((16 * groups, 192), BF16),
            pltpu.SemaphoreType.DMA((4,)),
            pltpu.SemaphoreType.DMA((5, 8)),
            pltpu.SemaphoreType.DMA((5, 8)),
            pltpu.SemaphoreType.DMA((groups,)),
            pltpu.SemaphoreType.DMA((groups,)),
        ],
        compiler_params=pltpu.CompilerParams(
            collective_id=0, has_side_effects=True, vmem_limit_bytes=32 * 1024 * 1024
        ),
    )(
        density,
        solid,
        load,
        start,
        stencil.transpose(1, 2, 0),
        owner.reshape(1, 64),
    )
    return disp, owned[None, None]


def solution(mesh):
    placed = (
        P("slab", "blk", None),
        P("slab", "blk", None),
        P(None, "slab", "blk", None),
        P(None, "slab", "blk", None),
        P(),
        P("slab", "blk", None, None),
    )
    return jax.shard_map(
        on_device,
        mesh=mesh,
        in_specs=placed,
        out_specs=(P(None, "slab", "blk", None), P("slab", "blk", None, None, None)),
        check_vma=False,
    )
```

```python
import functools

import jax
import jax.numpy as jnp
from jax import lax
from jax.experimental import pallas as pl
from jax.experimental.pallas import tpu as pltpu
from jax.sharding import PartitionSpec as P

OMEGA = 0.6
EMIN = 0.1
CAP = 10
MESH = pl.DeviceIdType.MESH
F32 = jnp.float32
BF16 = jnp.bfloat16
STAGE = 99
DIRS = ((1, 1), (1, -1), (-1, 1), (-1, -1), (0, 1), (0, -1), (1, 0), (-1, 0))
FAR = ((2, 1), (2, -1), (-2, 1), (-2, -1), (2, 0), (-2, 0))
HANDOUT = (12, 4, 11, 5, 13, 3, 10, 6, 14, 2, 9, 7, 8, 15, 1)


def iota(shape, dim):
    return lax.broadcasted_iota(jnp.int32, shape, dim)


def split2(value):
    high = value.astype(BF16).astype(F32)
    return high, value - high


def split3(value):
    high, rest = split2(value)
    mid, low = split2(rest)
    return high, mid, low


def lane_mod(lanes, size, count):
    for step in range(count, 0, -1):
        lanes = jnp.where(lanes >= size * step, lanes - size * step, lanes)
    return lanes


def band_position(window, wide, has_low, has_high):
    far = jnp.int32(-1000)
    low_off = jnp.where(has_low, jnp.int32(-16 - wide), far)
    high_off = jnp.where(has_high, jnp.int32(-wide), far)
    outside = jnp.where(window < 16 + wide, window + low_off, window + high_off)
    outside = jnp.where(window >= 16 + 2 * wide, far, outside)
    return jnp.where(window < 16, window, outside)


def band_matrix(st_ref, ex, rows_y, rows, wide, dilate, flags, scale, centre):
    lanes = iota((rows, 216), 1)
    window = lane_mod(lanes, 24, 8)
    position = band_position(window, wide, *flags)
    target = rows_y(iota((rows, 216), 0))
    masks = [position == target + dilate * (ey - 1) for ey in range(3)]
    lane_row = iota((1, 216), 1)
    in_comp = lane_mod(lane_row, 72, 2)
    first_comp, second_comp = in_comp < 24, in_comp < 48
    use_high = lanes < 144
    blocks = []
    for ez in range(3):
        for a in range(3):
            total = jnp.zeros((rows, 216), F32)
            for ey in range(3):
                off = 9 * ex + 3 * ey + ez
                coef = jnp.where(
                    first_comp,
                    st_ref[a, 0, off],
                    jnp.where(second_comp, st_ref[a, 1, off], st_ref[a, 2, off]),
                )
                if scale is not None:
                    coef = coef * scale[a]
                    if off == 13:
                        own = (in_comp >= 24 * a) & (in_comp < 24 * a + 24)
                        coef = coef + jnp.where(own, F32(centre), F32(0.0))
                total = jnp.where(masks[ey], coef, total)
            high, low = split2(total)
            blocks.append(jnp.where(use_high, high, low))
    return jnp.concatenate(blocks, axis=0).astype(BF16)


def stencil_apply(planes, mat_ref, rows, dilate):
    count = len(planes) - 2
    parts = []
    for plane in planes:
        high, low = split2(plane)
        parts.append(jnp.concatenate([high, low, high], axis=0).astype(BF16))
    total = None
    for ex in range(3):
        right = jnp.concatenate(parts[ex : ex + count], axis=1)
        piece = jnp.dot(mat_ref[ex], right, preferred_element_type=F32)
        total = piece if total is None else total + piece
    size = 3 * rows
    lanes = iota((size, 128), 1)
    result = []
    for x in range(count):
        down, mid, up = (
            total[ez * size : (ez + 1) * size, x * 128 : (x + 1) * 128] for ez in range(3)
        )
        down = jnp.where(lanes >= dilate, pltpu.roll(down, dilate, 1), 0.0)
        up = jnp.where(lanes < 128 - dilate, pltpu.roll(up, 128 - dilate, 1), 0.0)
        result.append(mid + down + up)
    return result


def smooth(planes, wy_ref, wz_ref):
    count = len(planes) - 8
    sums = []
    for x in range(count):
        v = planes[x : x + 9]
        sums.append(
            (v[0] + v[8])
            + 2.0 * (v[1] + v[7])
            + 3.0 * (v[2] + v[6])
            + 4.0 * (v[3] + v[5])
            + 5.0 * v[4]
        )
    stacked = jnp.concatenate(split3(jnp.concatenate(sums, axis=1)), axis=0).astype(BF16)
    cols = jnp.dot(wy_ref[...], stacked, preferred_element_type=F32)
    cols = jnp.concatenate([cols[:, x * 128 : (x + 1) * 128] for x in range(count)], axis=0)
    pair = jnp.concatenate(split2(cols), axis=1).astype(BF16)
    return jnp.dot(pair, wz_ref[...], preferred_element_type=F32)


def inner_and_ring(row):
    ring = jnp.where(row == 16, -1, jnp.where(row == 17, 16, -5000))
    return jnp.where(row < 16, row, ring)


def halo_planes(dx, width):
    if dx == 0:
        return 0, width, 4
    many = min(width - 4 * (abs(dx) - 1), 4)
    if dx > 0:
        return 4 - many, width - 4 * dx + 4 - many, many
    return 0, width - 4 * dx, many


def halo_rows(dy, width):
    if dy == 0:
        return 0, 0, 16
    return (16 - width, 16, width) if dy > 0 else (0, 16 + width, width)


def edge_weight(place, extent):
    def missing(n):
        n = jnp.maximum(n, 0)
        return lax.shift_right_logical(n * (n + 1), 1)

    weight = 25 - missing(4 - place) - missing(5 + place - extent)
    return jnp.maximum(weight, 1).astype(F32)


def pair_sum(value, axis, size):
    index = iota(value.shape, axis)
    even = lax.rem(index, 2) == 0
    return value + jnp.where(
        even, pltpu.roll(value, size - 1, axis), pltpu.roll(value, 1, axis)
    )


def kernel(
    slabs,
    groups,
    cap,
    density,
    solid,
    load,
    start,
    stencil,
    owner,
    disp_ref,
    owned_ref,
    st_ref,
    owner_v,
    dens_win,
    sens_win,
    f0,
    coarse,
    load_win,
    solid_win,
    packed,
    mat0,
    mat1,
    mat2,
    wy0_ref,
    wy1_ref,
    wz_ref,
    pick_ref,
    local_sem,
    send_sem,
    recv_sem,
    far_send,
    far_recv,
    give_sem,
    take_sem,
):
    p = lax.axis_index("slab")
    s = lax.axis_index("blk")

    def neighbour(dx, dy):
        return (lax.rem(p + dx + slabs, slabs), lax.rem(s + dy + groups, groups))

    partners = [neighbour(dx, dy) for dx, dy in FAR + DIRS if dx != 0]
    partners += [(p, lax.rem(s + d, groups)) for d in HANDOUT if d < groups]

    locals_ = [
        pltpu.make_async_copy(stencil, st_ref, local_sem.at[0]),
        pltpu.make_async_copy(owner, owner_v, local_sem.at[1]),
        pltpu.make_async_copy(start, f0.at[:, 2:6, 0:16], local_sem.at[2]),
        pltpu.make_async_copy(density, dens_win.at[5:9, 0:16], local_sem.at[3]),
        pltpu.make_async_copy(load, load_win.at[:, 1:5, 0:16], local_sem.at[4]),
        pltpu.make_async_copy(solid, solid_win.at[1:5, 0:16], local_sem.at[5]),
    ]
    f0[:, :, 16:24] = jnp.zeros((3, 8, 8, 128), F32)
    dens_win[:, 24:32] = jnp.zeros((14, 8, 128), F32)
    load_win[:, :, 16:24] = jnp.zeros((3, 6, 8, 128), F32)
    solid_win[:, 16:24] = jnp.zeros((6, 8, 128), jnp.int32)

    barrier = pltpu.get_barrier_semaphore()
    for partner in partners:
        pl.semaphore_signal(barrier, inc=1, device_id=partner, device_id_type=MESH)
    for copy in locals_:
        copy.start()
    pl.semaphore_wait(barrier, len(partners))

    started = []

    def window(src, dst, width, lead, base=0):
        def make(dx, dy):
            sx, tx, nx = halo_planes(dx, width)
            sy, ty, ny = halo_rows(dy, width)
            here = (pl.ds(base + sx, nx), pl.ds(sy, ny))
            there = (pl.ds(tx, nx), pl.ds(ty, ny))
            if lead:
                here, there = (slice(None), *here), (slice(None), *there)
            return src.at[here], dst.at[there]

        return make

    def coarse_window(fields):
        def make(dx, dy):
            sy, ty, ny = halo_rows(dy, 4)
            return (
                coarse.at[fields, 1, pl.ds(sy, ny)],
                coarse.at[fields, 1 - dx, pl.ds(ty, ny)],
            )

        return make

    def exchange(rows, far=None):
        copies = {row: [] for row, _ in rows}
        distant = []
        for i, (dx, dy) in enumerate(FAR if far is not None else ()):
            src, dst = far(dx, dy)
            distant.append(
                pltpu.make_async_remote_copy(
                    src_ref=src,
                    dst_ref=dst,
                    send_sem=far_send.at[i],
                    recv_sem=far_recv.at[i],
                    device_id=neighbour(dx, dy),
                    device_id_type=MESH,
                )
            )
            distant[-1].start()
        for i, (dx, dy) in enumerate(DIRS):
            for row, make in rows:
                src, dst = make(dx, dy)
                copies[row].append(
                    pltpu.make_async_remote_copy(
                        src_ref=src,
                        dst_ref=dst,
                        send_sem=send_sem.at[row, i],
                        recv_sem=recv_sem.at[row, i],
                        device_id=neighbour(dx, dy),
                        device_id_type=MESH,
                    )
                )
                copies[row][-1].start()
        everything = [c for group in copies.values() for c in group] + distant
        started.extend(everything)
        return everything

    def arrive(copies):
        for copy in copies:
            copy.wait_recv()

    def finish():
        disp_ref[...] = jnp.zeros_like(disp_ref)
        owned_ref[...] = jnp.zeros_like(owned_ref)
        for copy in started:
            copy.wait_send()

    far_dens = window(density, dens_win, 5, False)
    inputs = exchange(
        [
            (0, window(start, f0, 2, True)),
            (1, window(density, dens_win, 5, False)),
            (2, window(load, load_win, 1, True)),
            (3, window(solid, solid_win, 1, False)),
        ],
        far_dens,
    )

    flags = (s > 0, s < groups - 1)

    def switch(flag):
        return jnp.where(flag, 1.0, 0.0).astype(F32)

    mask_low, mask_high = switch(p > 0), switch(p < slabs - 1)
    far_low, far_high = switch(p > 1), switch(p < slabs - 2)
    locals_[0].wait()
    relax = [OMEGA / jnp.full((8, 128), st_ref[a, a, 13], F32)[0:1, :] for a in range(3)]
    tall = [-relax[a][:, 0:1] for a in range(3)]
    for ex in range(3):
        mat0[ex] = band_matrix(st_ref, ex, inner_and_ring, 24, 2, 1, flags, tall, 1.0)
    for ex in range(3):
        mat1[ex] = band_matrix(st_ref, ex, lambda r: r, 16, 1, 1, flags, None, 0.0)
    for ex in range(3):
        mat2[ex] = band_matrix(st_ref, ex, inner_and_ring, 24, 4, 2, flags, tall, 2.0)

    def triangle(distance):
        return jnp.maximum(5 - jnp.abs(distance), 0).astype(F32).astype(BF16)

    wy0_pos = band_position(lane_mod(iota((24, 96), 1), 32, 2), 5, *flags)
    wy0_ref[...] = triangle(wy0_pos - inner_and_ring(iota((24, 96), 0)))
    wy1_pos = band_position(lane_mod(iota((16, 72), 1), 24, 2), 4, *flags)
    wy1_ref[...] = triangle(wy1_pos - iota((16, 72), 0))
    wz_ref[...] = triangle(lane_mod(iota((256, 128), 0), 128, 1) - iota((256, 128), 1))
    row_y = inner_and_ring(iota((24, 128), 0))
    weight_yz = edge_weight(s * 16 + row_y, 16 * groups) * edge_weight(iota((24, 128), 1), 128)
    inv_weight = []
    for j in range(6):
        weight_x = edge_weight(jnp.full((24, 128), p * 4 + (j - 1), jnp.int32), 4 * slabs)
        inv_weight.append(1.0 / (weight_yz * weight_x))

    locals_[1].wait()
    names = owner_v[...].astype(F32)
    down, across = iota((64, 64), 0), iota((64, 64), 1)
    names_col = jnp.sum(jnp.where(down == across, names, 0.0), axis=1, keepdims=True)
    earlier = (names_col == names) & (across < down)
    rank = jnp.sum(jnp.where(earlier, 1.0, 0.0), axis=1, keepdims=True)
    code_col = names_col * 16.0 + rank
    spread = iota((64, 192), 0) == lane_mod(iota((64, 192), 1), 64, 2)
    code_row = jnp.sum(jnp.where(spread, code_col, 0.0), axis=0, keepdims=True)
    slot = iota((16 * groups, 192), 0).astype(F32)
    pick_ref[...] = jnp.where(slot == code_row, 1.0, 0.0).astype(BF16)

    for copy in locals_[2:]:
        copy.wait()
    if STAGE == 0:
        arrive(inputs)
        return finish()
    arrive(inputs)

    planes = [dens_win[j] for j in range(14)]
    for j, mask in enumerate([far_low] + [mask_low] * 4):
        planes[j] = planes[j] * mask
    for j, mask in enumerate([mask_high] * 4 + [far_high]):
        planes[9 + j] = planes[9 + j] * mask
    hfield = smooth(planes, wy0_ref, wz_ref)
    young, xphys = [], []
    for j in range(6):
        xphys.append(hfield[24 * j : 24 * j + 24] * inv_weight[j])
        solid_f = solid_win[j].astype(F32)
        young.append(EMIN + solid_f * (xphys[j] * xphys[j] * xphys[j]))
    lanes16 = iota((16, 128), 1)
    even_lane = lax.rem(lanes16, 2) == 0

    def coarsen(quarter):
        halves = [
            pair_sum(pair_sum(quarter[2 * i] + quarter[2 * i + 1], 1, 128), 0, 16) * 0.125
            for i in range(2)
        ]
        return jnp.where(even_lane, halves[0], halves[1])

    coarse[3, 1, 0:16] = coarsen([young[1 + x][0:16] for x in range(4)])
    young_in = exchange([(4, coarse_window(pl.ds(3, 1)))])
    planes = []
    for j in range(8):
        plane = f0[:, j].reshape(72, 128)
        planes.append(plane * mask_low if j < 2 else plane * mask_high if j > 5 else plane)
    relaxed = stencil_apply(planes, mat0, 24, 1)
    first = []
    for j in range(6):
        inv_young = 1.0 / young[j]
        push = jnp.concatenate(
            [relax[a] * (load_win[a, j] * inv_young) for a in range(3)], axis=0
        )
        first.append(relaxed[j] + push)

    def ends_masked(fields):
        return [fields[0] * mask_low, *fields[1:5], fields[5] * mask_high]

    s_first = stencil_apply(ends_masked(first), mat1, 16, 1)
    for a in range(3):
        coarse[a, 1, 0:16] = coarsen(
            [
                load_win[a, 1 + x, 0:16] - young[1 + x][0:16] * s_first[x][16 * a : 16 * a + 16]
                for x in range(4)
            ]
        )
    if STAGE == 1:
        arrive(young_in)
        return finish()
    coarse_in = exchange([(5, coarse_window(pl.ds(0, 3)))])
    sens_scale, out_scale = [], []
    for x in range(4):
        dens = dens_win[5 + x, 0:16]
        solid_f = solid_win[1 + x, 0:16].astype(F32)
        sens_scale.append((-3.0 * dens) * (xphys[1 + x][0:16] * xphys[1 + x][0:16]) * solid_f)
        out_scale.append(inv_weight[1 + x][0:16] / dens)
    arrive(young_in)
    arrive(coarse_in)
    if STAGE == 2:
        return finish()

    even72 = lax.rem(iota((24, 128), 1), 2) == 0
    corr_planes = []
    for plane in range(3):
        inv_cy = 1.0 / coarse[3, plane]
        both = [relax[a] * (coarse[a, plane] * inv_cy) for a in range(3)]
        if plane == 0:
            both = [v * mask_low for v in both]
        if plane == 2:
            both = [v * mask_high for v in both]
        lower = [jnp.where(even72, v, pltpu.roll(v, 1, 1)) for v in both]
        upper = [jnp.where(even72, pltpu.roll(v, 127, 1), v) for v in both]
        corr_planes.append(jnp.concatenate(lower, axis=0))
        corr_planes.append(jnp.concatenate(upper, axis=0))
    corr = stencil_apply(corr_planes, mat2, 24, 2)

    disp = [first[j] + corr[c] for j, c in enumerate((0, 1, 1, 2, 2, 3))]
    s_disp = stencil_apply(ends_masked(disp), mat1, 16, 1)
    for x in range(4):
        energy = None
        for a in range(3):
            term = disp[1 + x][24 * a : 24 * a + 16] * s_disp[x][16 * a : 16 * a + 16]
            energy = term if energy is None else energy + term
        sens_win[4 + x, 0:16] = sens_scale[x] * energy
    if STAGE == 3:
        return finish()
    sens_in = exchange([(6, window(sens_win, sens_win, 4, False, 4))])
    for x in range(4):
        for a in range(3):
            disp_ref[a, x] = disp[1 + x][24 * a : 24 * a + 16]
    arrive(sens_in)
    if STAGE == 4:
        return finish()
    planes = [sens_win[j] for j in range(12)]
    planes = [v * mask_low for v in planes[:4]] + planes[4:8] + [v * mask_high for v in planes[8:]]
    filtered = smooth(planes, wy1_ref, wz_ref) * jnp.concatenate(out_scale, axis=0)

    three = jnp.concatenate(split3(filtered), axis=0).astype(BF16)
    rows = jnp.dot(pick_ref[...], three, preferred_element_type=F32)
    for j in range(groups):
        packed[j] = rows[16 * j : 16 * j + cap]
    if STAGE == 5:
        return finish()
    gives = []
    for d in HANDOUT:
        if d >= groups:
            continue
        target = lax.rem(s + d, groups)
        gives.append(
            pltpu.make_async_remote_copy(
                src_ref=packed.at[target],
                dst_ref=owned_ref.at[s],
                send_sem=give_sem.at[d],
                recv_sem=take_sem.at[d],
                device_id=(p, target),
                device_id_type=MESH,
            )
        )
        gives[-1].start()
    owned_ref[s] = packed[s]
    arrive(gives)
    for copy in started + gives:
        copy.wait_send()


def on_device(density, solid, load, start, stencil, owner):
    slabs, groups = lax.axis_size("slab"), lax.axis_size("blk")
    cap = CAP
    hbm = pl.BlockSpec(memory_space=pltpu.HBM)
    vmem = pl.BlockSpec(memory_space=pltpu.VMEM)
    operands = (
        density,
        solid,
        load,
        start,
        stencil.transpose(1, 2, 0),
        owner.reshape(1, 64),
    )
    disp, owned = pl.pallas_call(
        functools.partial(kernel, slabs, groups, cap),
        out_shape=(
            pltpu.VMEM(load.shape, F32),
            pltpu.VMEM((groups, cap, 128), F32),
        ),
        in_specs=[hbm] * 6,
        out_specs=(vmem, vmem),
        scratch_shapes=[
            pltpu.SMEM((3, 3, 27), F32),
            pltpu.VMEM((1, 64), jnp.int32),
            pltpu.VMEM((14, 32, 128), F32),
            pltpu.VMEM((12, 24, 128), F32),
            pltpu.VMEM((3, 8, 24, 128), F32),
            pltpu.VMEM((4, 3, 24, 128), F32),
            pltpu.VMEM((3, 6, 24, 128), F32),
            pltpu.VMEM((6, 24, 128), jnp.int32),
            pltpu.VMEM((groups, cap, 128), F32),
            pltpu.VMEM((3, 216, 216), BF16),
            pltpu.VMEM((3, 144, 216), BF16),
            pltpu.VMEM((3, 216, 216), BF16),
            pltpu.VMEM((24, 96), BF16),
            pltpu.VMEM((16, 72), BF16),
            pltpu.VMEM((256, 128), BF16),
            pltpu.VMEM((16 * groups, 192), BF16),
            pltpu.SemaphoreType.DMA((6,)),
            pltpu.SemaphoreType.DMA((7, 8)),
            pltpu.SemaphoreType.DMA((7, 8)),
            pltpu.SemaphoreType.DMA((6,)),
            pltpu.SemaphoreType.DMA((6,)),
            pltpu.SemaphoreType.DMA((groups,)),
            pltpu.SemaphoreType.DMA((groups,)),
        ],
        compiler_params=pltpu.CompilerParams(
            collective_id=0, has_side_effects=True, vmem_limit_bytes=24 * 1024 * 1024
        ),
    )(*(pltpu.with_memory_space_constraint(x, pltpu.HBM) for x in operands))
    return disp, owned[None, None]


def solution(mesh):
    placed = (
        P("slab", "blk", None),
        P("slab", "blk", None),
        P(None, "slab", "blk", None),
        P(None, "slab", "blk", None),
        P(),
        P("slab", "blk", None, None),
    )
    return jax.shard_map(
        on_device,
        mesh=mesh,
        in_specs=placed,
        out_specs=(P(None, "slab", "blk", None), P("slab", "blk", None, None, None)),
        check_vma=False,
    )
```

```python
import functools

import jax
import jax.numpy as jnp
from jax import lax
from jax.experimental import pallas as pl
from jax.experimental.pallas import tpu as pltpu
from jax.sharding import PartitionSpec as P

OMEGA = 0.6
EMIN = 0.1
CAP = 10
MESH = pl.DeviceIdType.MESH
F32 = jnp.float32
BF16 = jnp.bfloat16
DIRS = ((1, 1), (1, -1), (-1, 1), (-1, -1), (0, 1), (0, -1), (1, 0), (-1, 0))
FAR = ((2, 1), (2, -1), (-2, 1), (-2, -1), (2, 0), (-2, 0))
HANDOUT = (12, 4, 11, 5, 13, 3, 10, 6, 14, 2, 9, 7, 8, 15, 1)


def iota(shape, dim):
    return lax.broadcasted_iota(jnp.int32, shape, dim)


def split2(value):
    high = value.astype(BF16).astype(F32)
    return high, value - high


def split3(value):
    high, rest = split2(value)
    mid, low = split2(rest)
    return high, mid, low


def lane_mod(lanes, size, count):
    for step in range(count, 0, -1):
        lanes = jnp.where(lanes >= size * step, lanes - size * step, lanes)
    return lanes


def band_position(window, wide, has_low, has_high):
    far = jnp.int32(-1000)
    low_off = jnp.where(has_low, jnp.int32(-16 - wide), far)
    high_off = jnp.where(has_high, jnp.int32(-wide), far)
    outside = jnp.where(window < 16 + wide, window + low_off, window + high_off)
    outside = jnp.where(window >= 16 + 2 * wide, far, outside)
    return jnp.where(window < 16, window, outside)


def band_matrix(st_ref, ex, rows_y, rows, wide, dilate, flags, scale, centre):
    lanes = iota((rows, 216), 1)
    window = lane_mod(lanes, 24, 8)
    position = band_position(window, wide, *flags)
    target = rows_y(iota((rows, 216), 0))
    masks = [position == target + dilate * (ey - 1) for ey in range(3)]
    lane_row = iota((1, 216), 1)
    in_comp = lane_mod(lane_row, 72, 2)
    first_comp, second_comp = in_comp < 24, in_comp < 48
    use_high = lanes < 144
    blocks = []
    for ez in range(3):
        for a in range(3):
            total = jnp.zeros((rows, 216), F32)
            for ey in range(3):
                off = 9 * ex + 3 * ey + ez
                coef = jnp.where(
                    first_comp,
                    st_ref[a, 0, off],
                    jnp.where(second_comp, st_ref[a, 1, off], st_ref[a, 2, off]),
                )
                if scale is not None:
                    coef = coef * scale[a]
                    if off == 13:
                        own = (in_comp >= 24 * a) & (in_comp < 24 * a + 24)
                        coef = coef + jnp.where(own, F32(centre), F32(0.0))
                total = jnp.where(masks[ey], coef, total)
            high, low = split2(total)
            blocks.append(jnp.where(use_high, high, low))
    return jnp.concatenate(blocks, axis=0).astype(BF16)


def stencil_apply(planes, mat_ref, rows, dilate):
    count = len(planes) - 2
    parts = []
    for plane in planes:
        high, low = split2(plane)
        parts.append(jnp.concatenate([high, low, high], axis=0).astype(BF16))
    total = None
    for ex in range(3):
        right = jnp.concatenate(parts[ex : ex + count], axis=1)
        piece = jnp.dot(mat_ref[ex], right, preferred_element_type=F32)
        total = piece if total is None else total + piece
    size = 3 * rows
    lanes = iota((size, 128), 1)
    result = []
    for x in range(count):
        down, mid, up = (
            total[ez * size : (ez + 1) * size, x * 128 : (x + 1) * 128] for ez in range(3)
        )
        down = jnp.where(lanes >= dilate, pltpu.roll(down, dilate, 1), 0.0)
        up = jnp.where(lanes < 128 - dilate, pltpu.roll(up, 128 - dilate, 1), 0.0)
        result.append(mid + down + up)
    return result


def smooth(planes, wy_ref, wz_ref):
    count = len(planes) - 8
    sums = []
    for x in range(count):
        v = planes[x : x + 9]
        sums.append(
            (v[0] + v[8])
            + 2.0 * (v[1] + v[7])
            + 3.0 * (v[2] + v[6])
            + 4.0 * (v[3] + v[5])
            + 5.0 * v[4]
        )
    stacked = jnp.concatenate(split3(jnp.concatenate(sums, axis=1)), axis=0).astype(BF16)
    cols = jnp.dot(wy_ref[...], stacked, preferred_element_type=F32)
    cols = jnp.concatenate([cols[:, x * 128 : (x + 1) * 128] for x in range(count)], axis=0)
    pair = jnp.concatenate(split2(cols), axis=1).astype(BF16)
    return jnp.dot(pair, wz_ref[...], preferred_element_type=F32)


def inner_and_ring(row):
    ring = jnp.where(row == 16, -1, jnp.where(row == 17, 16, -5000))
    return jnp.where(row < 16, row, ring)


def halo_planes(dx, width):
    if dx == 0:
        return 0, width, 4
    many = min(width - 4 * (abs(dx) - 1), 4)
    if dx > 0:
        return 4 - many, width - 4 * dx + 4 - many, many
    return 0, width - 4 * dx, many


def halo_rows(dy, width):
    if dy == 0:
        return 0, 0, 16
    return (16 - width, 16, width) if dy > 0 else (0, 16 + width, width)


def edge_weight(place, extent):
    def missing(n):
        n = jnp.maximum(n, 0)
        return lax.shift_right_logical(n * (n + 1), 1)

    weight = 25 - missing(4 - place) - missing(5 + place - extent)
    return jnp.maximum(weight, 1).astype(F32)


def pair_sum(value, axis, size):
    index = iota(value.shape, axis)
    even = lax.rem(index, 2) == 0
    return value + jnp.where(
        even, pltpu.roll(value, size - 1, axis), pltpu.roll(value, 1, axis)
    )


def kernel(
    slabs,
    groups,
    cap,
    density,
    solid,
    load,
    start,
    stencil,
    owner,
    disp_ref,
    owned_ref,
    st_ref,
    owner_v,
    dens_win,
    sens_win,
    f0,
    coarse,
    load_win,
    solid_win,
    packed,
    mat0,
    mat1,
    mat2,
    wy0_ref,
    wy1_ref,
    wz_ref,
    pick_ref,
    local_sem,
    send_sem,
    recv_sem,
    far_send,
    far_recv,
    give_sem,
    take_sem,
):
    p = lax.axis_index("slab")
    s = lax.axis_index("blk")

    def neighbour(dx, dy):
        return (lax.rem(p + dx + slabs, slabs), lax.rem(s + dy + groups, groups))

    inner = (p > 1) & (p < slabs - 2) & (s > 0) & (s < groups - 1)

    def each(pairs, act, receive=False):
        pairs = [((-dx, -dy) if receive else (dx, dy), entry) for (dx, dy), entry in pairs]

        @pl.when(inner)
        def _():
            for _, entry in pairs:
                act(entry)

        @pl.when(jnp.logical_not(inner))
        def _():
            for dx, dy in FAR + DIRS:
                group = [entry for where, entry in pairs if where == (dx, dy)]
                if group:
                    inside = (p + dx >= 0) & (p + dx < slabs) & (s + dy >= 0) & (s + dy < groups)

                    @pl.when(inside)
                    def _(group=group):
                        for entry in group:
                            act(entry)

    locals_ = [
        pltpu.make_async_copy(stencil, st_ref, local_sem.at[0]),
        pltpu.make_async_copy(owner, owner_v, local_sem.at[1]),
        pltpu.make_async_copy(start, f0.at[:, 2:6, 0:16], local_sem.at[2]),
        pltpu.make_async_copy(density, dens_win.at[5:9, 0:16], local_sem.at[3]),
        pltpu.make_async_copy(load, load_win.at[:, 1:5, 0:16], local_sem.at[4]),
        pltpu.make_async_copy(solid, solid_win.at[1:5, 0:16], local_sem.at[5]),
    ]
    f0[:, :, 16:24] = jnp.zeros((3, 8, 8, 128), F32)
    dens_win[:, 24:32] = jnp.zeros((14, 8, 128), F32)
    load_win[:, :, 16:24] = jnp.zeros((3, 6, 8, 128), F32)
    solid_win[:, 16:24] = jnp.zeros((6, 8, 128), jnp.int32)

    @pl.when(jnp.logical_not(inner))
    def _():
        f0[...] = jnp.zeros_like(f0)
        dens_win[...] = jnp.zeros_like(dens_win)
        load_win[...] = jnp.zeros_like(load_win)
        solid_win[...] = jnp.zeros_like(solid_win)
        sens_win[...] = jnp.zeros_like(sens_win)
        coarse[...] = jnp.ones_like(coarse)

    barrier = pltpu.get_barrier_semaphore()

    def greet(partner):
        pl.semaphore_signal(barrier, inc=1, device_id=partner, device_id_type=MESH)

    each([((dx, dy), neighbour(dx, dy)) for dx, dy in FAR + DIRS if dx != 0], greet)
    for d in HANDOUT:
        if d < groups:
            greet((p, lax.rem(s + d, groups)))
    for copy in locals_:
        copy.start()

    def count(flag):
        return jnp.where(flag, jnp.int32(1), jnp.int32(0))

    slabs_near = count(p > 0) + count(p < slabs - 1) + count(p > 1) + count(p < slabs - 2)
    pl.semaphore_wait(
        barrier, groups - 1 + slabs_near * (1 + count(s > 0) + count(s < groups - 1))
    )

    started = []

    def window(src, dst, width, lead, base=0):
        def make(dx, dy):
            sx, tx, nx = halo_planes(dx, width)
            sy, ty, ny = halo_rows(dy, width)
            here = (pl.ds(base + sx, nx), pl.ds(sy, ny))
            there = (pl.ds(tx, nx), pl.ds(ty, ny))
            if lead:
                here, there = (slice(None), *here), (slice(None), *there)
            return src.at[here], dst.at[there]

        return make

    def coarse_window(fields):
        def make(dx, dy):
            sy, ty, ny = halo_rows(dy, 4)
            return (
                coarse.at[fields, 1, pl.ds(sy, ny)],
                coarse.at[fields, 1 - dx, pl.ds(ty, ny)],
            )

        return make

    def exchange(rows, far=None):
        copies = []

        def add(src, dst, dx, dy, sems):
            copy = pltpu.make_async_remote_copy(
                src_ref=src,
                dst_ref=dst,
                send_sem=sems[0],
                recv_sem=sems[1],
                device_id=neighbour(dx, dy),
                device_id_type=MESH,
            )
            copies.append(((dx, dy), copy))

        for i, (dx, dy) in enumerate(FAR if far is not None else ()):
            add(*far(dx, dy), dx, dy, (far_send.at[i], far_recv.at[i]))
        for i, (dx, dy) in enumerate(DIRS):
            for row, make in rows:
                add(*make(dx, dy), dx, dy, (send_sem.at[row, i], recv_sem.at[row, i]))
        each(copies, lambda copy: copy.start())
        started.extend(copies)
        return copies

    def arrive(copies):
        each(copies, lambda copy: copy.wait_recv(), receive=True)

    far_dens = window(density, dens_win, 5, False)
    inputs = exchange(
        [
            (0, window(start, f0, 2, True)),
            (1, window(density, dens_win, 5, False)),
            (2, window(load, load_win, 1, True)),
            (3, window(solid, solid_win, 1, False)),
        ],
        far_dens,
    )

    flags = (s > 0, s < groups - 1)

    def switch(flag):
        return jnp.where(flag, 1.0, 0.0).astype(F32)

    mask_low, mask_high = switch(p > 0), switch(p < slabs - 1)
    locals_[0].wait()
    relax = [OMEGA / jnp.full((8, 128), st_ref[a, a, 13], F32)[0:1, :] for a in range(3)]
    tall = [-relax[a][:, 0:1] for a in range(3)]
    for ex in range(3):
        mat0[ex] = band_matrix(st_ref, ex, inner_and_ring, 24, 2, 1, flags, tall, 1.0)
    for ex in range(3):
        mat1[ex] = band_matrix(st_ref, ex, lambda r: r, 16, 1, 1, flags, None, 0.0)
    for ex in range(3):
        mat2[ex] = band_matrix(st_ref, ex, inner_and_ring, 24, 4, 2, flags, tall, 2.0)

    def triangle(distance):
        return jnp.maximum(5 - jnp.abs(distance), 0).astype(F32).astype(BF16)

    wy0_pos = band_position(lane_mod(iota((24, 96), 1), 32, 2), 5, *flags)
    wy0_ref[...] = triangle(wy0_pos - inner_and_ring(iota((24, 96), 0)))
    wy1_pos = band_position(lane_mod(iota((16, 72), 1), 24, 2), 4, *flags)
    wy1_ref[...] = triangle(wy1_pos - iota((16, 72), 0))
    wz_ref[...] = triangle(lane_mod(iota((256, 128), 0), 128, 1) - iota((256, 128), 1))
    row_y = inner_and_ring(iota((24, 128), 0))
    weight_yz = edge_weight(s * 16 + row_y, 16 * groups) * edge_weight(iota((24, 128), 1), 128)
    inv_weight = []
    for j in range(6):
        weight_x = edge_weight(jnp.full((24, 128), p * 4 + (j - 1), jnp.int32), 4 * slabs)
        inv_weight.append(1.0 / (weight_yz * weight_x))

    locals_[1].wait()
    names = owner_v[...].astype(F32)
    down, across = iota((64, 64), 0), iota((64, 64), 1)
    names_col = jnp.sum(jnp.where(down == across, names, 0.0), axis=1, keepdims=True)
    earlier = (names_col == names) & (across < down)
    rank = jnp.sum(jnp.where(earlier, 1.0, 0.0), axis=1, keepdims=True)
    code_col = names_col * 16.0 + rank
    spread = iota((64, 192), 0) == lane_mod(iota((64, 192), 1), 64, 2)
    code_row = jnp.sum(jnp.where(spread, code_col, 0.0), axis=0, keepdims=True)
    slot = iota((16 * groups, 192), 0).astype(F32)
    pick_ref[...] = jnp.where(slot == code_row, 1.0, 0.0).astype(BF16)

    for copy in locals_[2:6]:
        copy.wait()
    arrive(inputs)

    hfield = smooth([dens_win[j] for j in range(14)], wy0_ref, wz_ref)
    young, xphys = [], []
    for j in range(6):
        xphys.append(hfield[24 * j : 24 * j + 24] * inv_weight[j])
        solid_f = solid_win[j].astype(F32)
        young.append(EMIN + solid_f * (xphys[j] * xphys[j] * xphys[j]))
    lanes16 = iota((16, 128), 1)
    even_lane = lax.rem(lanes16, 2) == 0

    def coarsen(quarter):
        halves = [
            pair_sum(pair_sum(quarter[2 * i] + quarter[2 * i + 1], 1, 128), 0, 16) * 0.125
            for i in range(2)
        ]
        return jnp.where(even_lane, halves[0], halves[1])

    coarse[3, 1, 0:16] = coarsen([young[1 + x][0:16] for x in range(4)])
    young_in = exchange([(4, coarse_window(pl.ds(3, 1)))])
    relaxed = stencil_apply([f0[:, j].reshape(72, 128) for j in range(8)], mat0, 24, 1)
    first = []
    for j in range(6):
        inv_young = 1.0 / young[j]
        push = jnp.concatenate(
            [relax[a] * (load_win[a, j] * inv_young) for a in range(3)], axis=0
        )
        first.append(relaxed[j] + push)

    def ends_masked(fields):
        return [fields[0] * mask_low, *fields[1:5], fields[5] * mask_high]

    s_first = stencil_apply(ends_masked(first), mat1, 16, 1)
    for a in range(3):
        coarse[a, 1, 0:16] = coarsen(
            [
                load_win[a, 1 + x, 0:16] - young[1 + x][0:16] * s_first[x][16 * a : 16 * a + 16]
                for x in range(4)
            ]
        )
    coarse_in = exchange([(5, coarse_window(pl.ds(0, 3)))])
    sens_scale, out_scale = [], []
    for x in range(4):
        dens = dens_win[5 + x, 0:16]
        solid_f = solid_win[1 + x, 0:16].astype(F32)
        sens_scale.append((-3.0 * dens) * (xphys[1 + x][0:16] * xphys[1 + x][0:16]) * solid_f)
        out_scale.append(inv_weight[1 + x][0:16] / dens)
    arrive(young_in)
    arrive(coarse_in)

    even72 = lax.rem(iota((24, 128), 1), 2) == 0
    corr_planes = []
    for plane in range(3):
        inv_cy = 1.0 / coarse[3, plane]
        both = [relax[a] * (coarse[a, plane] * inv_cy) for a in range(3)]
        if plane == 0:
            both = [v * mask_low for v in both]
        if plane == 2:
            both = [v * mask_high for v in both]
        lower = [jnp.where(even72, v, pltpu.roll(v, 1, 1)) for v in both]
        upper = [jnp.where(even72, pltpu.roll(v, 127, 1), v) for v in both]
        corr_planes.append(jnp.concatenate(lower, axis=0))
        corr_planes.append(jnp.concatenate(upper, axis=0))
    corr = stencil_apply(corr_planes, mat2, 24, 2)

    disp = [first[j] + corr[c] for j, c in enumerate((0, 1, 1, 2, 2, 3))]
    s_disp = stencil_apply(ends_masked(disp), mat1, 16, 1)
    for x in range(4):
        energy = None
        for a in range(3):
            term = disp[1 + x][24 * a : 24 * a + 16] * s_disp[x][16 * a : 16 * a + 16]
            energy = term if energy is None else energy + term
        sens_win[4 + x, 0:16] = sens_scale[x] * energy
    sens_in = exchange([(6, window(sens_win, sens_win, 4, False, 4))])
    for x in range(4):
        for a in range(3):
            disp_ref[a, x] = disp[1 + x][24 * a : 24 * a + 16]
    arrive(sens_in)
    filtered = smooth([sens_win[j] for j in range(12)], wy1_ref, wz_ref) * jnp.concatenate(out_scale, axis=0)

    three = jnp.concatenate(split3(filtered), axis=0).astype(BF16)
    rows = jnp.dot(pick_ref[...], three, preferred_element_type=F32)
    for j in range(groups):
        packed[j] = rows[16 * j : 16 * j + cap]
    gives = []
    for d in HANDOUT:
        if d >= groups:
            continue
        target = lax.rem(s + d, groups)
        gives.append(
            pltpu.make_async_remote_copy(
                src_ref=packed.at[target],
                dst_ref=owned_ref.at[:, s],
                send_sem=give_sem.at[d],
                recv_sem=take_sem.at[d],
                device_id=(p, target),
                device_id_type=MESH,
            )
        )
        gives[-1].start()
    own = pltpu.make_async_copy(packed.at[s], owned_ref.at[:, s], local_sem.at[6])
    own.start()
    for copy in gives:
        copy.wait_recv()
    own.wait()
    for copy in gives:
        copy.wait_send()
    each(started, lambda copy: copy.wait_send())


def hand_out(disp_in, owned_in, disp_out, owned_out, sems):
    copies = [
        pltpu.make_async_copy(disp_in, disp_out, sems.at[0]),
        pltpu.make_async_copy(owned_in, owned_out, sems.at[1]),
    ]
    for copy in copies:
        copy.start()
    for copy in copies:
        copy.wait()


def on_device(density, solid, load, start, stencil, owner):
    slabs, groups = lax.axis_size("slab"), lax.axis_size("blk")
    cap = CAP
    hbm = pl.BlockSpec(memory_space=pltpu.HBM)
    vmem = pl.BlockSpec(memory_space=pltpu.VMEM)
    operands = (
        density,
        solid,
        load,
        start,
        stencil.transpose(1, 2, 0),
        owner.reshape(1, 64),
    )
    disp, owned = pl.pallas_call(
        functools.partial(kernel, slabs, groups, cap),
        out_shape=(
            pltpu.VMEM(load.shape, F32),
            pltpu.VMEM((cap, groups, 128), F32),
        ),
        in_specs=[hbm] * 6,
        out_specs=(vmem, vmem),
        scratch_shapes=[
            pltpu.SMEM((3, 3, 27), F32),
            pltpu.VMEM((1, 64), jnp.int32),
            pltpu.VMEM((14, 32, 128), F32),
            pltpu.VMEM((12, 24, 128), F32),
            pltpu.VMEM((3, 8, 24, 128), F32),
            pltpu.VMEM((4, 3, 24, 128), F32),
            pltpu.VMEM((3, 6, 24, 128), F32),
            pltpu.VMEM((6, 24, 128), jnp.int32),
            pltpu.VMEM((groups, cap, 128), F32),
            pltpu.VMEM((3, 216, 216), BF16),
            pltpu.VMEM((3, 144, 216), BF16),
            pltpu.VMEM((3, 216, 216), BF16),
            pltpu.VMEM((24, 96), BF16),
            pltpu.VMEM((16, 72), BF16),
            pltpu.VMEM((256, 128), BF16),
            pltpu.VMEM((16 * groups, 192), BF16),
            pltpu.SemaphoreType.DMA((7,)),
            pltpu.SemaphoreType.DMA((7, 8)),
            pltpu.SemaphoreType.DMA((7, 8)),
            pltpu.SemaphoreType.DMA((6,)),
            pltpu.SemaphoreType.DMA((6,)),
            pltpu.SemaphoreType.DMA((groups,)),
            pltpu.SemaphoreType.DMA((groups,)),
        ],
        compiler_params=pltpu.CompilerParams(
            collective_id=0, has_side_effects=True, vmem_limit_bytes=24 * 1024 * 1024
        ),
    )(*(pltpu.with_memory_space_constraint(x, pltpu.HBM) for x in operands))
    disp, owned = pl.pallas_call(
        hand_out,
        out_shape=(jax.ShapeDtypeStruct(disp.shape, F32), jax.ShapeDtypeStruct(owned.shape, F32)),
        in_specs=[vmem, vmem],
        out_specs=(hbm, hbm),
        scratch_shapes=[pltpu.SemaphoreType.DMA((2,))],
        compiler_params=pltpu.CompilerParams(vmem_limit_bytes=8 * 1024 * 1024),
    )(*(pltpu.with_memory_space_constraint(x, pltpu.VMEM) for x in (disp, owned)))
    return disp, owned.transpose(1, 0, 2)[None, None]


def solution(mesh):
    placed = (
        P("slab", "blk", None),
        P("slab", "blk", None),
        P(None, "slab", "blk", None),
        P(None, "slab", "blk", None),
        P(),
        P("slab", "blk", None, None),
    )
    return jax.shard_map(
        on_device,
        mesh=mesh,
        in_specs=placed,
        out_specs=(P(None, "slab", "blk", None), P("slab", "blk", None, None, None)),
        check_vma=False,
    )
```

```python
import functools

import jax
import jax.numpy as jnp
from jax import lax
from jax.experimental import pallas as pl
from jax.experimental.pallas import tpu as pltpu
from jax.sharding import PartitionSpec as P

OMEGA = 0.6
EMIN = 0.1
CAP = 10
MESH = pl.DeviceIdType.MESH
F32 = jnp.float32
BF16 = jnp.bfloat16
DIRS = ((1, 1), (1, -1), (-1, 1), (-1, -1), (0, 1), (0, -1), (1, 0), (-1, 0))
FAR = ((2, 1), (2, -1), (-2, 1), (-2, -1), (2, 0), (-2, 0))
HANDOUT = (12, 4, 11, 5, 13, 3, 10, 6, 14, 2, 9, 7, 8, 15, 1)


def iota(shape, dim):
    return lax.broadcasted_iota(jnp.int32, shape, dim)


def split2(value):
    high = value.astype(BF16).astype(F32)
    return high, value - high


def split3(value):
    high, rest = split2(value)
    mid, low = split2(rest)
    return high, mid, low


def lane_mod(lanes, size, count):
    for step in range(count, 0, -1):
        lanes = jnp.where(lanes >= size * step, lanes - size * step, lanes)
    return lanes


def band_position(window, wide, has_low, has_high):
    far = jnp.int32(-1000)
    low_off = jnp.where(has_low, jnp.int32(-16 - wide), far)
    high_off = jnp.where(has_high, jnp.int32(-wide), far)
    outside = jnp.where(window < 16 + wide, window + low_off, window + high_off)
    outside = jnp.where(window >= 16 + 2 * wide, far, outside)
    return jnp.where(window < 16, window, outside)


def band_matrix(st_ref, ex, rows_y, rows, wide, dilate, flags, scale, centre):
    lanes = iota((rows, 216), 1)
    window = lane_mod(lanes, 24, 8)
    position = band_position(window, wide, *flags)
    target = rows_y(iota((rows, 216), 0))
    masks = [position == target + dilate * (ey - 1) for ey in range(3)]
    lane_row = iota((1, 216), 1)
    in_comp = lane_mod(lane_row, 72, 2)
    first_comp, second_comp = in_comp < 24, in_comp < 48
    use_high = lanes < 144
    blocks = []
    for ez in range(3):
        for a in range(3):
            total = jnp.zeros((rows, 216), F32)
            for ey in range(3):
                off = 9 * ex + 3 * ey + ez
                coef = jnp.where(
                    first_comp,
                    st_ref[a, 0, off],
                    jnp.where(second_comp, st_ref[a, 1, off], st_ref[a, 2, off]),
                )
                if scale is not None:
                    coef = coef * scale[a]
                    if off == 13:
                        own = (in_comp >= 24 * a) & (in_comp < 24 * a + 24)
                        coef = coef + jnp.where(own, F32(centre), F32(0.0))
                total = jnp.where(masks[ey], coef, total)
            high, low = split2(total)
            blocks.append(jnp.where(use_high, high, low))
    return jnp.concatenate(blocks, axis=0).astype(BF16)


def stencil_apply(planes, mat_ref, rows, dilate):
    count = len(planes) - 2
    parts = []
    for plane in planes:
        high, low = split2(plane)
        parts.append(jnp.concatenate([high, low, high], axis=0).astype(BF16))
    total = None
    for ex in range(3):
        right = jnp.concatenate(parts[ex : ex + count], axis=1)
        piece = jnp.dot(mat_ref[ex], right, preferred_element_type=F32)
        total = piece if total is None else total + piece
    size = 3 * rows
    lanes = iota((size, 128), 1)
    result = []
    for x in range(count):
        down, mid, up = (
            total[ez * size : (ez + 1) * size, x * 128 : (x + 1) * 128] for ez in range(3)
        )
        down = jnp.where(lanes >= dilate, pltpu.roll(down, dilate, 1), 0.0)
        up = jnp.where(lanes < 128 - dilate, pltpu.roll(up, 128 - dilate, 1), 0.0)
        result.append(mid + down + up)
    return result


def smooth(planes, wy_ref, wz_ref):
    count = len(planes) - 8
    sums = []
    for x in range(count):
        v = planes[x : x + 9]
        sums.append(
            (v[0] + v[8])
            + 2.0 * (v[1] + v[7])
            + 3.0 * (v[2] + v[6])
            + 4.0 * (v[3] + v[5])
            + 5.0 * v[4]
        )
    stacked = jnp.concatenate(split3(jnp.concatenate(sums, axis=1)), axis=0).astype(BF16)
    cols = jnp.dot(wy_ref[...], stacked, preferred_element_type=F32)
    cols = jnp.concatenate([cols[:, x * 128 : (x + 1) * 128] for x in range(count)], axis=0)
    pair = jnp.concatenate(split2(cols), axis=1).astype(BF16)
    return jnp.dot(pair, wz_ref[...], preferred_element_type=F32)


def inner_and_ring(row):
    ring = jnp.where(row == 16, -1, jnp.where(row == 17, 16, -5000))
    return jnp.where(row < 16, row, ring)


def halo_planes(dx, width):
    if dx == 0:
        return 0, width, 4
    many = min(width - 4 * (abs(dx) - 1), 4)
    if dx > 0:
        return 4 - many, width - 4 * dx + 4 - many, many
    return 0, width - 4 * dx, many


def halo_rows(dy, width):
    if dy == 0:
        return 0, 0, 16
    return (16 - width, 16, width) if dy > 0 else (0, 16 + width, width)


def edge_weight(place, extent):
    def missing(n):
        n = jnp.maximum(n, 0)
        return lax.shift_right_logical(n * (n + 1), 1)

    weight = 25 - missing(4 - place) - missing(5 + place - extent)
    return jnp.maximum(weight, 1).astype(F32)


def pair_sum(value, axis, size):
    index = iota(value.shape, axis)
    even = lax.rem(index, 2) == 0
    return value + jnp.where(
        even, pltpu.roll(value, size - 1, axis), pltpu.roll(value, 1, axis)
    )


def kernel(
    slabs,
    groups,
    cap,
    density,
    solid,
    load,
    start,
    stencil,
    owner,
    disp_ref,
    owned_ref,
    st_ref,
    owner_v,
    dens_win,
    sens_win,
    f0,
    coarse,
    load_win,
    solid_win,
    packed,
    mat0,
    mat1,
    mat2,
    wy0_ref,
    wy1_ref,
    wz_ref,
    pick_ref,
    local_sem,
    send_sem,
    recv_sem,
    far_send,
    far_recv,
    give_sem,
    take_sem,
    token_sem,
):
    p = lax.axis_index("slab")
    s = lax.axis_index("blk")

    def neighbour(dx, dy):
        return (lax.rem(p + dx + slabs, slabs), lax.rem(s + dy + groups, groups))

    inner = (p > 1) & (p < slabs - 2) & (s > 0) & (s < groups - 1)

    def each(pairs, act, receive=False):
        pairs = [((-dx, -dy) if receive else (dx, dy), entry) for (dx, dy), entry in pairs]

        @pl.when(inner)
        def _():
            for _, entry in pairs:
                act(entry)

        @pl.when(jnp.logical_not(inner))
        def _():
            for dx, dy in FAR + DIRS:
                group = [entry for where, entry in pairs if where == (dx, dy)]
                if group:
                    inside = (p + dx >= 0) & (p + dx < slabs) & (s + dy >= 0) & (s + dy < groups)

                    @pl.when(inside)
                    def _(group=group):
                        for entry in group:
                            act(entry)

    locals_ = [
        pltpu.make_async_copy(stencil, st_ref, local_sem.at[0]),
        pltpu.make_async_copy(owner, owner_v, local_sem.at[1]),
        pltpu.make_async_copy(start, f0.at[:, 2:6, 0:16], local_sem.at[2]),
        pltpu.make_async_copy(density, dens_win.at[5:9, 0:16], local_sem.at[3]),
        pltpu.make_async_copy(load, load_win.at[:, 1:5, 0:16], local_sem.at[4]),
        pltpu.make_async_copy(solid, solid_win.at[1:5, 0:16], local_sem.at[5]),
    ]
    f0[:, :, 16:24] = jnp.zeros((3, 8, 8, 128), F32)
    dens_win[:, 24:32] = jnp.zeros((14, 8, 128), F32)
    load_win[:, :, 16:24] = jnp.zeros((3, 6, 8, 128), F32)
    solid_win[:, 16:24] = jnp.zeros((6, 8, 128), jnp.int32)

    @pl.when(jnp.logical_not(inner))
    def _():
        f0[...] = jnp.zeros_like(f0)
        dens_win[...] = jnp.zeros_like(dens_win)
        load_win[...] = jnp.zeros_like(load_win)
        solid_win[...] = jnp.zeros_like(solid_win)
        sens_win[...] = jnp.zeros_like(sens_win)
        coarse[...] = jnp.ones_like(coarse)

    barrier = pltpu.get_barrier_semaphore()

    def greet(partner):
        pl.semaphore_signal(barrier, inc=1, device_id=partner, device_id_type=MESH)

    each([((dx, dy), neighbour(dx, dy)) for dx, dy in FAR + DIRS if dx != 0], greet)
    for d in (1, groups - 1):
        greet((p, lax.rem(s + d, groups)))
    for copy in locals_:
        copy.start()

    def count(flag):
        return jnp.where(flag, jnp.int32(1), jnp.int32(0))

    slabs_near = count(p > 0) + count(p < slabs - 1) + count(p > 1) + count(p < slabs - 2)
    pl.semaphore_wait(
        barrier, 2 + slabs_near * (1 + count(s > 0) + count(s < groups - 1))
    )

    started = []

    def window(src, dst, width, lead, base=0):
        def make(dx, dy):
            sx, tx, nx = halo_planes(dx, width)
            sy, ty, ny = halo_rows(dy, width)
            here = (pl.ds(base + sx, nx), pl.ds(sy, ny))
            there = (pl.ds(tx, nx), pl.ds(ty, ny))
            if lead:
                here, there = (slice(None), *here), (slice(None), *there)
            return src.at[here], dst.at[there]

        return make

    def coarse_window(fields):
        def make(dx, dy):
            sy, ty, ny = halo_rows(dy, 4)
            return (
                coarse.at[fields, 1, pl.ds(sy, ny)],
                coarse.at[fields, 1 - dx, pl.ds(ty, ny)],
            )

        return make

    def exchange(rows, far=None):
        copies = []

        def add(src, dst, dx, dy, sems):
            copy = pltpu.make_async_remote_copy(
                src_ref=src,
                dst_ref=dst,
                send_sem=sems[0],
                recv_sem=sems[1],
                device_id=neighbour(dx, dy),
                device_id_type=MESH,
            )
            copies.append(((dx, dy), copy))

        for i, (dx, dy) in enumerate(FAR if far is not None else ()):
            add(*far(dx, dy), dx, dy, (far_send.at[i], far_recv.at[i]))
        for i, (dx, dy) in enumerate(DIRS):
            for row, make in rows:
                add(*make(dx, dy), dx, dy, (send_sem.at[row, i], recv_sem.at[row, i]))
        each(copies, lambda copy: copy.start())
        started.extend(copies)
        return copies

    def arrive(copies):
        each(copies, lambda copy: copy.wait_recv(), receive=True)

    def tell(stage):
        reach = 2**stage
        if 2 * reach < groups:
            for d in (reach, groups - reach):
                pl.semaphore_signal(
                    token_sem.at[stage],
                    inc=1,
                    device_id=(p, lax.rem(s + d, groups)),
                    device_id_type=MESH,
                )

    def hear(stage):
        if 2 * 2**stage < groups:
            pl.semaphore_wait(token_sem.at[stage], 2)

    far_dens = window(density, dens_win, 5, False)
    inputs = exchange(
        [
            (0, window(start, f0, 2, True)),
            (1, window(density, dens_win, 5, False)),
            (2, window(load, load_win, 1, True)),
            (3, window(solid, solid_win, 1, False)),
        ],
        far_dens,
    )

    tell(0)

    flags = (s > 0, s < groups - 1)

    def switch(flag):
        return jnp.where(flag, 1.0, 0.0).astype(F32)

    mask_low, mask_high = switch(p > 0), switch(p < slabs - 1)
    locals_[0].wait()
    relax = [OMEGA / jnp.full((8, 128), st_ref[a, a, 13], F32)[0:1, :] for a in range(3)]
    tall = [-relax[a][:, 0:1] for a in range(3)]
    for ex in range(3):
        mat0[ex] = band_matrix(st_ref, ex, inner_and_ring, 24, 2, 1, flags, tall, 1.0)
    for ex in range(3):
        mat1[ex] = band_matrix(st_ref, ex, lambda r: r, 16, 1, 1, flags, None, 0.0)
    for ex in range(3):
        mat2[ex] = band_matrix(st_ref, ex, inner_and_ring, 24, 4, 2, flags, tall, 2.0)

    def triangle(distance):
        return jnp.maximum(5 - jnp.abs(distance), 0).astype(F32).astype(BF16)

    wy0_pos = band_position(lane_mod(iota((24, 96), 1), 32, 2), 5, *flags)
    wy0_ref[...] = triangle(wy0_pos - inner_and_ring(iota((24, 96), 0)))
    wy1_pos = band_position(lane_mod(iota((16, 72), 1), 24, 2), 4, *flags)
    wy1_ref[...] = triangle(wy1_pos - iota((16, 72), 0))
    wz_ref[...] = triangle(lane_mod(iota((256, 128), 0), 128, 1) - iota((256, 128), 1))
    row_y = inner_and_ring(iota((24, 128), 0))
    weight_yz = edge_weight(s * 16 + row_y, 16 * groups) * edge_weight(iota((24, 128), 1), 128)
    inv_weight = []
    for j in range(6):
        weight_x = edge_weight(jnp.full((24, 128), p * 4 + (j - 1), jnp.int32), 4 * slabs)
        inv_weight.append(1.0 / (weight_yz * weight_x))

    locals_[1].wait()
    names = owner_v[...].astype(F32)
    down, across = iota((64, 64), 0), iota((64, 64), 1)
    names_col = jnp.sum(jnp.where(down == across, names, 0.0), axis=1, keepdims=True)
    earlier = (names_col == names) & (across < down)
    rank = jnp.sum(jnp.where(earlier, 1.0, 0.0), axis=1, keepdims=True)
    code_col = names_col * 16.0 + rank
    spread = iota((64, 192), 0) == lane_mod(iota((64, 192), 1), 64, 2)
    code_row = jnp.sum(jnp.where(spread, code_col, 0.0), axis=0, keepdims=True)
    slot = iota((16 * groups, 192), 0).astype(F32)
    pick_ref[...] = jnp.where(slot == code_row, 1.0, 0.0).astype(BF16)

    for copy in locals_[2:6]:
        copy.wait()
    arrive(inputs)
    hear(0)
    tell(1)

    hfield = smooth([dens_win[j] for j in range(14)], wy0_ref, wz_ref)
    young, xphys = [], []
    for j in range(6):
        xphys.append(hfield[24 * j : 24 * j + 24] * inv_weight[j])
        solid_f = solid_win[j].astype(F32)
        young.append(EMIN + solid_f * (xphys[j] * xphys[j] * xphys[j]))
    lanes16 = iota((16, 128), 1)
    even_lane = lax.rem(lanes16, 2) == 0

    def coarsen(quarter):
        halves = [
            pair_sum(pair_sum(quarter[2 * i] + quarter[2 * i + 1], 1, 128), 0, 16) * 0.125
            for i in range(2)
        ]
        return jnp.where(even_lane, halves[0], halves[1])

    coarse[3, 1, 0:16] = coarsen([young[1 + x][0:16] for x in range(4)])
    young_in = exchange([(4, coarse_window(pl.ds(3, 1)))])
    relaxed = stencil_apply([f0[:, j].reshape(72, 128) for j in range(8)], mat0, 24, 1)
    first = []
    for j in range(6):
        inv_young = 1.0 / young[j]
        push = jnp.concatenate(
            [relax[a] * (load_win[a, j] * inv_young) for a in range(3)], axis=0
        )
        first.append(relaxed[j] + push)

    def ends_masked(fields):
        return [fields[0] * mask_low, *fields[1:5], fields[5] * mask_high]

    s_first = stencil_apply(ends_masked(first), mat1, 16, 1)
    for a in range(3):
        coarse[a, 1, 0:16] = coarsen(
            [
                load_win[a, 1 + x, 0:16] - young[1 + x][0:16] * s_first[x][16 * a : 16 * a + 16]
                for x in range(4)
            ]
        )
    coarse_in = exchange([(5, coarse_window(pl.ds(0, 3)))])
    sens_scale, out_scale = [], []
    for x in range(4):
        dens = dens_win[5 + x, 0:16]
        solid_f = solid_win[1 + x, 0:16].astype(F32)
        sens_scale.append((-3.0 * dens) * (xphys[1 + x][0:16] * xphys[1 + x][0:16]) * solid_f)
        out_scale.append(inv_weight[1 + x][0:16] / dens)
    arrive(young_in)
    arrive(coarse_in)
    hear(1)
    tell(2)

    even72 = lax.rem(iota((24, 128), 1), 2) == 0
    corr_planes = []
    for plane in range(3):
        inv_cy = 1.0 / coarse[3, plane]
        both = [relax[a] * (coarse[a, plane] * inv_cy) for a in range(3)]
        if plane == 0:
            both = [v * mask_low for v in both]
        if plane == 2:
            both = [v * mask_high for v in both]
        lower = [jnp.where(even72, v, pltpu.roll(v, 1, 1)) for v in both]
        upper = [jnp.where(even72, pltpu.roll(v, 127, 1), v) for v in both]
        corr_planes.append(jnp.concatenate(lower, axis=0))
        corr_planes.append(jnp.concatenate(upper, axis=0))
    corr = stencil_apply(corr_planes, mat2, 24, 2)

    disp = [first[j] + corr[c] for j, c in enumerate((0, 1, 1, 2, 2, 3))]
    s_disp = stencil_apply(ends_masked(disp), mat1, 16, 1)
    for x in range(4):
        energy = None
        for a in range(3):
            term = disp[1 + x][24 * a : 24 * a + 16] * s_disp[x][16 * a : 16 * a + 16]
            energy = term if energy is None else energy + term
        sens_win[4 + x, 0:16] = sens_scale[x] * energy
    sens_in = exchange([(6, window(sens_win, sens_win, 4, False, 4))])
    for x in range(4):
        for a in range(3):
            disp_ref[a, x] = disp[1 + x][24 * a : 24 * a + 16]
    arrive(sens_in)
    hear(2)
    filtered = smooth([sens_win[j] for j in range(12)], wy1_ref, wz_ref) * jnp.concatenate(out_scale, axis=0)

    three = jnp.concatenate(split3(filtered), axis=0).astype(BF16)
    rows = jnp.dot(pick_ref[...], three, preferred_element_type=F32)
    for j in range(groups):
        packed[j] = rows[16 * j : 16 * j + cap]
    gives = []
    for d in HANDOUT:
        if d >= groups:
            continue
        target = lax.rem(s + d, groups)
        gives.append(
            pltpu.make_async_remote_copy(
                src_ref=packed.at[target],
                dst_ref=owned_ref.at[:, s],
                send_sem=give_sem.at[d],
                recv_sem=take_sem.at[d],
                device_id=(p, target),
                device_id_type=MESH,
            )
        )
        gives[-1].start()
    own = pltpu.make_async_copy(packed.at[s], owned_ref.at[:, s], local_sem.at[6])
    own.start()
    for copy in gives:
        copy.wait_recv()
    own.wait()
    for copy in gives:
        copy.wait_send()
    each(started, lambda copy: copy.wait_send())


def hand_out(disp_in, owned_in, disp_out, owned_out, sems):
    copies = [
        pltpu.make_async_copy(disp_in, disp_out, sems.at[0]),
        pltpu.make_async_copy(owned_in, owned_out, sems.at[1]),
    ]
    for copy in copies:
        copy.start()
    for copy in copies:
        copy.wait()


def on_device(density, solid, load, start, stencil, owner):
    slabs, groups = lax.axis_size("slab"), lax.axis_size("blk")
    cap = CAP
    hbm = pl.BlockSpec(memory_space=pltpu.HBM)
    vmem = pl.BlockSpec(memory_space=pltpu.VMEM)
    operands = (
        density,
        solid,
        load,
        start,
        stencil.transpose(1, 2, 0),
        owner.reshape(1, 64),
    )
    disp, owned = pl.pallas_call(
        functools.partial(kernel, slabs, groups, cap),
        out_shape=(
            pltpu.VMEM(load.shape, F32),
            pltpu.VMEM((cap, groups, 128), F32),
        ),
        in_specs=[hbm] * 6,
        out_specs=(vmem, vmem),
        scratch_shapes=[
            pltpu.SMEM((3, 3, 27), F32),
            pltpu.VMEM((1, 64), jnp.int32),
            pltpu.VMEM((14, 32, 128), F32),
            pltpu.VMEM((12, 24, 128), F32),
            pltpu.VMEM((3, 8, 24, 128), F32),
            pltpu.VMEM((4, 3, 24, 128), F32),
            pltpu.VMEM((3, 6, 24, 128), F32),
            pltpu.VMEM((6, 24, 128), jnp.int32),
            pltpu.VMEM((groups, cap, 128), F32),
            pltpu.VMEM((3, 216, 216), BF16),
            pltpu.VMEM((3, 144, 216), BF16),
            pltpu.VMEM((3, 216, 216), BF16),
            pltpu.VMEM((24, 96), BF16),
            pltpu.VMEM((16, 72), BF16),
            pltpu.VMEM((256, 128), BF16),
            pltpu.VMEM((16 * groups, 192), BF16),
            pltpu.SemaphoreType.DMA((7,)),
            pltpu.SemaphoreType.DMA((7, 8)),
            pltpu.SemaphoreType.DMA((7, 8)),
            pltpu.SemaphoreType.DMA((6,)),
            pltpu.SemaphoreType.DMA((6,)),
            pltpu.SemaphoreType.DMA((groups,)),
            pltpu.SemaphoreType.DMA((groups,)),
            pltpu.SemaphoreType.REGULAR((3,)),
        ],
        compiler_params=pltpu.CompilerParams(
            collective_id=0, has_side_effects=True, vmem_limit_bytes=24 * 1024 * 1024
        ),
    )(*(pltpu.with_memory_space_constraint(x, pltpu.HBM) for x in operands))
    disp, owned = pl.pallas_call(
        hand_out,
        out_shape=(jax.ShapeDtypeStruct(disp.shape, F32), jax.ShapeDtypeStruct(owned.shape, F32)),
        in_specs=[vmem, vmem],
        out_specs=(hbm, hbm),
        scratch_shapes=[pltpu.SemaphoreType.DMA((2,))],
        compiler_params=pltpu.CompilerParams(vmem_limit_bytes=8 * 1024 * 1024),
    )(*(pltpu.with_memory_space_constraint(x, pltpu.VMEM) for x in (disp, owned)))
    return disp, owned.transpose(1, 0, 2)[None, None]


def solution(mesh):
    placed = (
        P("slab", "blk", None),
        P("slab", "blk", None),
        P(None, "slab", "blk", None),
        P(None, "slab", "blk", None),
        P(),
        P("slab", "blk", None, None),
    )
    return jax.shard_map(
        on_device,
        mesh=mesh,
        in_specs=placed,
        out_specs=(P(None, "slab", "blk", None), P("slab", "blk", None, None, None)),
        check_vma=False,
    )
```

```python
import functools

import jax
import jax.numpy as jnp
from jax import lax
from jax.experimental import pallas as pl
from jax.experimental.pallas import tpu as pltpu
from jax.sharding import PartitionSpec as P

OMEGA = 0.6
EMIN = 0.1
CAP = 10
MESH = pl.DeviceIdType.MESH
F32 = jnp.float32
BF16 = jnp.bfloat16
DIRS = ((1, 1), (1, -1), (-1, 1), (-1, -1), (0, 1), (0, -1), (1, 0), (-1, 0))
FAR = ((2, 1), (2, -1), (-2, 1), (-2, -1), (2, 0), (-2, 0))
HANDOUT = (12, 4, 11, 5, 13, 3, 10, 6, 14, 2, 9, 7, 8, 15, 1)


def iota(shape, dim):
    return lax.broadcasted_iota(jnp.int32, shape, dim)


def split2(value):
    high = value.astype(BF16).astype(F32)
    return high, value - high


def split3(value):
    high, rest = split2(value)
    mid, low = split2(rest)
    return high, mid, low


def lane_mod(lanes, size, count):
    for step in range(count, 0, -1):
        lanes = jnp.where(lanes >= size * step, lanes - size * step, lanes)
    return lanes


def band_position(window, wide, has_low, has_high):
    far = jnp.int32(-1000)
    low_off = jnp.where(has_low, jnp.int32(-16 - wide), far)
    high_off = jnp.where(has_high, jnp.int32(-wide), far)
    outside = jnp.where(window < 16 + wide, window + low_off, window + high_off)
    outside = jnp.where(window >= 16 + 2 * wide, far, outside)
    return jnp.where(window < 16, window, outside)


def band_matrix(st_ref, ex, rows_y, rows, wide, dilate, flags, scale, centre):
    lanes = iota((rows, 216), 1)
    window = lane_mod(lanes, 24, 8)
    position = band_position(window, wide, *flags)
    target = rows_y(iota((rows, 216), 0))
    masks = [position == target + dilate * (ey - 1) for ey in range(3)]
    lane_row = iota((1, 216), 1)
    in_comp = lane_mod(lane_row, 72, 2)
    first_comp, second_comp = in_comp < 24, in_comp < 48
    use_high = lanes < 144
    blocks = []
    for ez in range(3):
        for a in range(3):
            total = jnp.zeros((rows, 216), F32)
            for ey in range(3):
                off = 9 * ex + 3 * ey + ez
                coef = jnp.where(
                    first_comp,
                    st_ref[a, 0, off],
                    jnp.where(second_comp, st_ref[a, 1, off], st_ref[a, 2, off]),
                )
                if scale is not None:
                    coef = coef * scale[a]
                    if off == 13:
                        own = (in_comp >= 24 * a) & (in_comp < 24 * a + 24)
                        coef = coef + jnp.where(own, F32(centre), F32(0.0))
                total = jnp.where(masks[ey], coef, total)
            high, low = split2(total)
            blocks.append(jnp.where(use_high, high, low))
    return jnp.concatenate(blocks, axis=0).astype(BF16)


def stencil_apply(planes, mat_ref, rows, dilate):
    count = len(planes) - 2
    parts = []
    for plane in planes:
        high, low = split2(plane)
        parts.append(jnp.concatenate([high, low, high], axis=0).astype(BF16))
    total = None
    for ex in range(3):
        right = jnp.concatenate(parts[ex : ex + count], axis=1)
        piece = jnp.dot(mat_ref[ex], right, preferred_element_type=F32)
        total = piece if total is None else total + piece
    size = 3 * rows
    lanes = iota((size, 128), 1)
    result = []
    for x in range(count):
        down, mid, up = (
            total[ez * size : (ez + 1) * size, x * 128 : (x + 1) * 128] for ez in range(3)
        )
        down = jnp.where(lanes >= dilate, pltpu.roll(down, dilate, 1), 0.0)
        up = jnp.where(lanes < 128 - dilate, pltpu.roll(up, 128 - dilate, 1), 0.0)
        result.append(mid + down + up)
    return result


def smooth(planes, wy_ref, wz_ref):
    count = len(planes) - 8
    sums = []
    for x in range(count):
        v = planes[x : x + 9]
        sums.append(
            (v[0] + v[8])
            + 2.0 * (v[1] + v[7])
            + 3.0 * (v[2] + v[6])
            + 4.0 * (v[3] + v[5])
            + 5.0 * v[4]
        )
    stacked = jnp.concatenate(split3(jnp.concatenate(sums, axis=1)), axis=0).astype(BF16)
    cols = jnp.dot(wy_ref[...], stacked, preferred_element_type=F32)
    cols = jnp.concatenate([cols[:, x * 128 : (x + 1) * 128] for x in range(count)], axis=0)
    pair = jnp.concatenate(split2(cols), axis=1).astype(BF16)
    return jnp.dot(pair, wz_ref[...], preferred_element_type=F32)


def inner_and_ring(row):
    ring = jnp.where(row == 16, -1, jnp.where(row == 17, 16, -5000))
    return jnp.where(row < 16, row, ring)


def halo_planes(dx, width):
    if dx == 0:
        return 0, width, 4
    many = min(width - 4 * (abs(dx) - 1), 4)
    if dx > 0:
        return 4 - many, width - 4 * dx + 4 - many, many
    return 0, width - 4 * dx, many


def halo_rows(dy, width):
    if dy == 0:
        return 0, 0, 16
    return (16 - width, 16, width) if dy > 0 else (0, 16 + width, width)


def edge_weight(place, extent):
    def missing(n):
        n = jnp.maximum(n, 0)
        return lax.shift_right_logical(n * (n + 1), 1)

    weight = 25 - missing(4 - place) - missing(5 + place - extent)
    return jnp.maximum(weight, 1).astype(F32)


def pair_sum(value, axis, size):
    index = iota(value.shape, axis)
    even = lax.rem(index, 2) == 0
    return value + jnp.where(
        even, pltpu.roll(value, size - 1, axis), pltpu.roll(value, 1, axis)
    )


def kernel(
    slabs,
    groups,
    cap,
    density,
    solid,
    load,
    start,
    stencil,
    owner,
    disp_ref,
    owned_ref,
    st_ref,
    owner_v,
    dens_win,
    sens_win,
    f0,
    coarse,
    load_win,
    solid_win,
    packed,
    mat0,
    mat1,
    mat2,
    wy0_ref,
    wy1_ref,
    wz_ref,
    pick_ref,
    local_sem,
    send_sem,
    recv_sem,
    far_send,
    far_recv,
    give_sem,
    take_sem,
    token_sem,
):
    p = lax.axis_index("slab")
    s = lax.axis_index("blk")

    def neighbour(dx, dy):
        return (lax.rem(p + dx + slabs, slabs), lax.rem(s + dy + groups, groups))

    inner = (p > 1) & (p < slabs - 2) & (s > 0) & (s < groups - 1)

    def each(pairs, act, receive=False):
        pairs = [((-dx, -dy) if receive else (dx, dy), entry) for (dx, dy), entry in pairs]

        @pl.when(inner)
        def _():
            for _, entry in pairs:
                act(entry)

        @pl.when(jnp.logical_not(inner))
        def _():
            for dx, dy in FAR + DIRS:
                group = [entry for where, entry in pairs if where == (dx, dy)]
                if group:
                    inside = (p + dx >= 0) & (p + dx < slabs) & (s + dy >= 0) & (s + dy < groups)

                    @pl.when(inside)
                    def _(group=group):
                        for entry in group:
                            act(entry)

    locals_ = [
        pltpu.make_async_copy(stencil, st_ref, local_sem.at[0]),
        pltpu.make_async_copy(owner, owner_v, local_sem.at[1]),
        pltpu.make_async_copy(start, f0.at[:, 2:6, 0:16], local_sem.at[2]),
        pltpu.make_async_copy(density, dens_win.at[5:9, 0:16], local_sem.at[3]),
        pltpu.make_async_copy(load, load_win.at[:, 1:5, 0:16], local_sem.at[4]),
        pltpu.make_async_copy(solid, solid_win.at[1:5, 0:16], local_sem.at[5]),
    ]
    f0[:, :, 16:24] = jnp.zeros((3, 8, 8, 128), F32)
    dens_win[:, 24:32] = jnp.zeros((14, 8, 128), F32)
    load_win[:, :, 16:24] = jnp.zeros((3, 6, 8, 128), F32)
    solid_win[:, 16:24] = jnp.zeros((6, 8, 128), jnp.int32)

    @pl.when(jnp.logical_not(inner))
    def _():
        f0[...] = jnp.zeros_like(f0)
        dens_win[...] = jnp.zeros_like(dens_win)
        load_win[...] = jnp.zeros_like(load_win)
        solid_win[...] = jnp.zeros_like(solid_win)
        sens_win[...] = jnp.zeros_like(sens_win)
        coarse[...] = jnp.ones_like(coarse)

    barrier = pltpu.get_barrier_semaphore()

    def greet(partner):
        pl.semaphore_signal(barrier, inc=1, device_id=partner, device_id_type=MESH)

    each([((dx, dy), neighbour(dx, dy)) for dx, dy in FAR + DIRS if dx != 0], greet)
    for d in (1, groups - 1):
        greet((p, lax.rem(s + d, groups)))
    for copy in locals_:
        copy.start()

    def count(flag):
        return jnp.where(flag, jnp.int32(1), jnp.int32(0))

    slabs_near = count(p > 0) + count(p < slabs - 1) + count(p > 1) + count(p < slabs - 2)
    pl.semaphore_wait(
        barrier, 2 + slabs_near * (1 + count(s > 0) + count(s < groups - 1))
    )

    started = []

    def window(src, dst, width, lead, base=0):
        def make(dx, dy):
            sx, tx, nx = halo_planes(dx, width)
            sy, ty, ny = halo_rows(dy, width)
            here = (pl.ds(base + sx, nx), pl.ds(sy, ny))
            there = (pl.ds(tx, nx), pl.ds(ty, ny))
            if lead:
                here, there = (slice(None), *here), (slice(None), *there)
            return src.at[here], dst.at[there]

        return make

    def coarse_window(fields):
        def make(dx, dy):
            sy, ty, ny = halo_rows(dy, 4)
            return (
                coarse.at[fields, 1, pl.ds(sy, ny)],
                coarse.at[fields, 1 - dx, pl.ds(ty, ny)],
            )

        return make

    def exchange(rows, far=None):
        copies = []
        by_row = {row: [] for row, _ in rows}

        def add(src, dst, dx, dy, sems):
            copy = pltpu.make_async_remote_copy(
                src_ref=src,
                dst_ref=dst,
                send_sem=sems[0],
                recv_sem=sems[1],
                device_id=neighbour(dx, dy),
                device_id_type=MESH,
            )
            copies.append(((dx, dy), copy))
            return copies[-1]

        for i, (dx, dy) in enumerate(FAR if far is not None else ()):
            add(*far(dx, dy), dx, dy, (far_send.at[i], far_recv.at[i]))
        near = list(enumerate(DIRS))
        order = [(where, entry) for where in near[:6] for entry in rows]
        order += [(where, entry) for entry in rows for where in near[6:]]
        for (i, (dx, dy)), (row, make) in order:
            sems = (send_sem.at[row, i], recv_sem.at[row, i])
            by_row[row].append(add(*make(dx, dy), dx, dy, sems))
        each(copies, lambda copy: copy.start())
        started.extend(copies)
        return by_row, copies[: len(FAR)]

    def arrive(copies):
        each(copies[::-1], lambda copy: copy.wait_recv(), receive=True)

    def tell(stage):
        reach = 2**stage
        if 2 * reach < groups:
            for d in (reach, groups - reach):
                pl.semaphore_signal(
                    token_sem.at[stage],
                    inc=1,
                    device_id=(p, lax.rem(s + d, groups)),
                    device_id_type=MESH,
                )

    def hear(stage):
        if 2 * 2**stage < groups:
            pl.semaphore_wait(token_sem.at[stage], 2)

    far_dens = window(density, dens_win, 5, False)
    inputs, far_in = exchange(
        [
            (1, window(density, dens_win, 5, False)),
            (3, window(solid, solid_win, 1, False)),
            (0, window(start, f0, 2, True)),
            (2, window(load, load_win, 1, True)),
        ],
        far_dens,
    )
    tell(0)

    flags = (s > 0, s < groups - 1)

    def switch(flag):
        return jnp.where(flag, 1.0, 0.0).astype(F32)

    mask_low, mask_high = switch(p > 0), switch(p < slabs - 1)
    locals_[0].wait()
    relax = [OMEGA / jnp.full((8, 128), st_ref[a, a, 13], F32)[0:1, :] for a in range(3)]
    tall = [-relax[a][:, 0:1] for a in range(3)]
    for ex in range(3):
        mat0[ex] = band_matrix(st_ref, ex, inner_and_ring, 24, 2, 1, flags, tall, 1.0)
    for ex in range(3):
        mat1[ex] = band_matrix(st_ref, ex, lambda r: r, 16, 1, 1, flags, None, 0.0)
    for ex in range(3):
        mat2[ex] = band_matrix(st_ref, ex, inner_and_ring, 24, 4, 2, flags, tall, 2.0)

    def triangle(distance):
        return jnp.maximum(5 - jnp.abs(distance), 0).astype(F32).astype(BF16)

    wy0_pos = band_position(lane_mod(iota((24, 96), 1), 32, 2), 5, *flags)
    wy0_ref[...] = triangle(wy0_pos - inner_and_ring(iota((24, 96), 0)))
    wy1_pos = band_position(lane_mod(iota((16, 72), 1), 24, 2), 4, *flags)
    wy1_ref[...] = triangle(wy1_pos - iota((16, 72), 0))
    wz_ref[...] = triangle(lane_mod(iota((256, 128), 0), 128, 1) - iota((256, 128), 1))
    row_y = inner_and_ring(iota((24, 128), 0))
    weight_yz = edge_weight(s * 16 + row_y, 16 * groups) * edge_weight(iota((24, 128), 1), 128)
    inv_weight = []
    for j in range(6):
        weight_x = edge_weight(jnp.full((24, 128), p * 4 + (j - 1), jnp.int32), 4 * slabs)
        inv_weight.append(1.0 / (weight_yz * weight_x))

    locals_[1].wait()
    names = owner_v[...].astype(F32)
    down, across = iota((64, 64), 0), iota((64, 64), 1)
    names_col = jnp.sum(jnp.where(down == across, names, 0.0), axis=1, keepdims=True)
    earlier = (names_col == names) & (across < down)
    rank = jnp.sum(jnp.where(earlier, 1.0, 0.0), axis=1, keepdims=True)
    code_col = names_col * 16.0 + rank
    spread = iota((64, 192), 0) == lane_mod(iota((64, 192), 1), 64, 2)
    code_row = jnp.sum(jnp.where(spread, code_col, 0.0), axis=0, keepdims=True)
    slot = iota((16 * groups, 192), 0).astype(F32)
    pick_ref[...] = jnp.where(slot == code_row, 1.0, 0.0).astype(BF16)

    for copy in locals_[2:6]:
        copy.wait()
    arrive(far_in + inputs[1] + inputs[3])

    hfield = smooth([dens_win[j] for j in range(14)], wy0_ref, wz_ref)
    young, xphys = [], []
    for j in range(6):
        xphys.append(hfield[24 * j : 24 * j + 24] * inv_weight[j])
        solid_f = solid_win[j].astype(F32)
        young.append(EMIN + solid_f * (xphys[j] * xphys[j] * xphys[j]))
    lanes16 = iota((16, 128), 1)
    even_lane = lax.rem(lanes16, 2) == 0

    def coarsen(quarter):
        halves = [
            pair_sum(pair_sum(quarter[2 * i] + quarter[2 * i + 1], 1, 128), 0, 16) * 0.125
            for i in range(2)
        ]
        return jnp.where(even_lane, halves[0], halves[1])

    coarse[3, 1, 0:16] = coarsen([young[1 + x][0:16] for x in range(4)])
    young_in = exchange([(4, coarse_window(pl.ds(3, 1)))])[0][4]
    arrive(inputs[0])
    relaxed = stencil_apply([f0[:, j].reshape(72, 128) for j in range(8)], mat0, 24, 1)
    arrive(inputs[2])
    hear(0)
    tell(1)
    first = []
    for j in range(6):
        inv_young = 1.0 / young[j]
        push = jnp.concatenate(
            [relax[a] * (load_win[a, j] * inv_young) for a in range(3)], axis=0
        )
        first.append(relaxed[j] + push)

    def ends_masked(fields):
        return [fields[0] * mask_low, *fields[1:5], fields[5] * mask_high]

    s_first = stencil_apply(ends_masked(first), mat1, 16, 1)
    for a in range(3):
        coarse[a, 1, 0:16] = coarsen(
            [
                load_win[a, 1 + x, 0:16] - young[1 + x][0:16] * s_first[x][16 * a : 16 * a + 16]
                for x in range(4)
            ]
        )
    coarse_in = exchange([(5, coarse_window(pl.ds(0, 3)))])[0][5]
    sens_scale, out_scale = [], []
    for x in range(4):
        dens = dens_win[5 + x, 0:16]
        solid_f = solid_win[1 + x, 0:16].astype(F32)
        sens_scale.append((-3.0 * dens) * (xphys[1 + x][0:16] * xphys[1 + x][0:16]) * solid_f)
        out_scale.append(inv_weight[1 + x][0:16] / dens)
    arrive(young_in)
    arrive(coarse_in)
    hear(1)
    tell(2)

    even72 = lax.rem(iota((24, 128), 1), 2) == 0
    corr_planes = []
    for plane in range(3):
        inv_cy = 1.0 / coarse[3, plane]
        both = [relax[a] * (coarse[a, plane] * inv_cy) for a in range(3)]
        if plane == 0:
            both = [v * mask_low for v in both]
        if plane == 2:
            both = [v * mask_high for v in both]
        lower = [jnp.where(even72, v, pltpu.roll(v, 1, 1)) for v in both]
        upper = [jnp.where(even72, pltpu.roll(v, 127, 1), v) for v in both]
        corr_planes.append(jnp.concatenate(lower, axis=0))
        corr_planes.append(jnp.concatenate(upper, axis=0))
    corr = stencil_apply(corr_planes, mat2, 24, 2)

    disp = [first[j] + corr[c] for j, c in enumerate((0, 1, 1, 2, 2, 3))]
    corr_fine = [corr[c] for c in (0, 1, 1, 2, 2, 3)]
    s_corr = stencil_apply(ends_masked(corr_fine), mat1, 16, 1)
    s_disp = [s_first[x] + s_corr[x] for x in range(4)]
    for x in range(4):
        energy = None
        for a in range(3):
            term = disp[1 + x][24 * a : 24 * a + 16] * s_disp[x][16 * a : 16 * a + 16]
            energy = term if energy is None else energy + term
        sens_win[4 + x, 0:16] = sens_scale[x] * energy
    sens_in = exchange([(6, window(sens_win, sens_win, 4, False, 4))])[0][6]
    for x in range(4):
        for a in range(3):
            disp_ref[a, x] = disp[1 + x][24 * a : 24 * a + 16]
    arrive(sens_in)
    hear(2)
    filtered = smooth([sens_win[j] for j in range(12)], wy1_ref, wz_ref) * jnp.concatenate(out_scale, axis=0)

    three = jnp.concatenate(split3(filtered), axis=0).astype(BF16)
    rows = jnp.dot(pick_ref[...], three, preferred_element_type=F32)
    for j in range(groups):
        packed[j] = rows[16 * j : 16 * j + cap]
    gives = []
    for d in HANDOUT:
        if d >= groups:
            continue
        target = lax.rem(s + d, groups)
        gives.append(
            pltpu.make_async_remote_copy(
                src_ref=packed.at[target],
                dst_ref=owned_ref.at[:, s],
                send_sem=give_sem.at[d],
                recv_sem=take_sem.at[d],
                device_id=(p, target),
                device_id_type=MESH,
            )
        )
        gives[-1].start()
    own = pltpu.make_async_copy(packed.at[s], owned_ref.at[:, s], local_sem.at[6])
    own.start()
    own.wait()
    each(started, lambda copy: copy.wait_send())
    for copy in gives:
        copy.wait_send()
    for copy in gives[::-1]:
        copy.wait_recv()


def hand_out(disp_in, owned_in, disp_out, owned_out, sems):
    copies = [
        pltpu.make_async_copy(disp_in, disp_out, sems.at[0]),
        pltpu.make_async_copy(owned_in, owned_out, sems.at[1]),
    ]
    for copy in copies:
        copy.start()
    for copy in copies:
        copy.wait()


def on_device(density, solid, load, start, stencil, owner):
    slabs, groups = lax.axis_size("slab"), lax.axis_size("blk")
    cap = CAP
    hbm = pl.BlockSpec(memory_space=pltpu.HBM)
    vmem = pl.BlockSpec(memory_space=pltpu.VMEM)
    operands = (
        density,
        solid,
        load,
        start,
        stencil.transpose(1, 2, 0),
        owner.reshape(1, 64),
    )
    disp, owned = pl.pallas_call(
        functools.partial(kernel, slabs, groups, cap),
        out_shape=(
            pltpu.VMEM(load.shape, F32),
            pltpu.VMEM((cap, groups, 128), F32),
        ),
        in_specs=[hbm] * 6,
        out_specs=(vmem, vmem),
        scratch_shapes=[
            pltpu.SMEM((3, 3, 27), F32),
            pltpu.VMEM((1, 64), jnp.int32),
            pltpu.VMEM((14, 32, 128), F32),
            pltpu.VMEM((12, 24, 128), F32),
            pltpu.VMEM((3, 8, 24, 128), F32),
            pltpu.VMEM((4, 3, 24, 128), F32),
            pltpu.VMEM((3, 6, 24, 128), F32),
            pltpu.VMEM((6, 24, 128), jnp.int32),
            pltpu.VMEM((groups, cap, 128), F32),
            pltpu.VMEM((3, 216, 216), BF16),
            pltpu.VMEM((3, 144, 216), BF16),
            pltpu.VMEM((3, 216, 216), BF16),
            pltpu.VMEM((24, 96), BF16),
            pltpu.VMEM((16, 72), BF16),
            pltpu.VMEM((256, 128), BF16),
            pltpu.VMEM((16 * groups, 192), BF16),
            pltpu.SemaphoreType.DMA((7,)),
            pltpu.SemaphoreType.DMA((7, 8)),
            pltpu.SemaphoreType.DMA((7, 8)),
            pltpu.SemaphoreType.DMA((6,)),
            pltpu.SemaphoreType.DMA((6,)),
            pltpu.SemaphoreType.DMA((groups,)),
            pltpu.SemaphoreType.DMA((groups,)),
            pltpu.SemaphoreType.REGULAR((3,)),
        ],
        compiler_params=pltpu.CompilerParams(
            collective_id=0, has_side_effects=True, vmem_limit_bytes=24 * 1024 * 1024
        ),
    )(*(pltpu.with_memory_space_constraint(x, pltpu.HBM) for x in operands))
    disp, owned = pl.pallas_call(
        hand_out,
        out_shape=(jax.ShapeDtypeStruct(disp.shape, F32), jax.ShapeDtypeStruct(owned.shape, F32)),
        in_specs=[vmem, vmem],
        out_specs=(hbm, hbm),
        scratch_shapes=[pltpu.SemaphoreType.DMA((2,))],
        compiler_params=pltpu.CompilerParams(vmem_limit_bytes=8 * 1024 * 1024),
    )(*(pltpu.with_memory_space_constraint(x, pltpu.VMEM) for x in (disp, owned)))
    return disp, owned.transpose(1, 0, 2)[None, None]


def solution(mesh):
    placed = (
        P("slab", "blk", None),
        P("slab", "blk", None),
        P(None, "slab", "blk", None),
        P(None, "slab", "blk", None),
        P(),
        P("slab", "blk", None, None),
    )
    return jax.shard_map(
        on_device,
        mesh=mesh,
        in_specs=placed,
        out_specs=(P(None, "slab", "blk", None), P("slab", "blk", None, None, None)),
        check_vma=False,
    )
```

```python
import functools

import jax
import jax.numpy as jnp
from jax import lax
from jax.experimental import pallas as pl
from jax.experimental.pallas import tpu as pltpu
from jax.sharding import PartitionSpec as P

OMEGA = 0.6
EMIN = 0.1
CAP = 10
MESH = pl.DeviceIdType.MESH
F32 = jnp.float32
BF16 = jnp.bfloat16
DIRS = ((1, 1), (1, -1), (-1, 1), (-1, -1), (0, 1), (0, -1), (1, 0), (-1, 0))
FAR = ((2, 1), (2, -1), (-2, 1), (-2, -1), (2, 0), (-2, 0))
HANDOUT = (12, 4, 11, 5, 13, 3, 10, 6, 14, 2, 9, 7, 8, 15, 1)


def iota(shape, dim):
    return lax.broadcasted_iota(jnp.int32, shape, dim)


def split2(value):
    high = value.astype(BF16).astype(F32)
    return high, value - high


def split3(value):
    high, rest = split2(value)
    mid, low = split2(rest)
    return high, mid, low


def lane_mod(lanes, size, count):
    for step in range(count, 0, -1):
        lanes = jnp.where(lanes >= size * step, lanes - size * step, lanes)
    return lanes


def band_position(window, wide, has_low, has_high):
    far = jnp.int32(-1000)
    low_off = jnp.where(has_low, jnp.int32(-16 - wide), far)
    high_off = jnp.where(has_high, jnp.int32(-wide), far)
    outside = jnp.where(window < 16 + wide, window + low_off, window + high_off)
    outside = jnp.where(window >= 16 + 2 * wide, far, outside)
    return jnp.where(window < 16, window, outside)


def band_matrix(st_ref, ex, rows_y, rows, wide, dilate, flags, scale, centre):
    lanes = iota((rows, 216), 1)
    window = lane_mod(lanes, 24, 8)
    position = band_position(window, wide, *flags)
    target = rows_y(iota((rows, 216), 0))
    masks = [position == target + dilate * (ey - 1) for ey in range(3)]
    lane_row = iota((1, 216), 1)
    in_comp = lane_mod(lane_row, 72, 2)
    first_comp, second_comp = in_comp < 24, in_comp < 48
    use_high = lanes < 144
    blocks = []
    for ez in range(3):
        for a in range(3):
            total = jnp.zeros((rows, 216), F32)
            for ey in range(3):
                off = 9 * ex + 3 * ey + ez
                coef = jnp.where(
                    first_comp,
                    st_ref[a, 0, off],
                    jnp.where(second_comp, st_ref[a, 1, off], st_ref[a, 2, off]),
                )
                if scale is not None:
                    coef = coef * scale[a]
                    if off == 13:
                        own = (in_comp >= 24 * a) & (in_comp < 24 * a + 24)
                        coef = coef + jnp.where(own, F32(centre), F32(0.0))
                total = jnp.where(masks[ey], coef, total)
            high, low = split2(total)
            blocks.append(jnp.where(use_high, high, low))
    return jnp.concatenate(blocks, axis=0).astype(BF16)


def stencil_apply(planes, mat_ref, rows, dilate):
    count = len(planes) - 2
    parts = []
    for plane in planes:
        high, low = split2(plane)
        parts.append(jnp.concatenate([high, low, high], axis=0).astype(BF16))
    sums = [None] * count
    for first in range(0, count + 2, 2):
        right = jnp.concatenate(parts[first : first + 2], axis=1)
        for ex in range(3):
            if not any(0 <= first + k - ex < count for k in range(2)):
                continue
            piece = jnp.dot(mat_ref[ex], right, preferred_element_type=F32)
            for k in range(2):
                x = first + k - ex
                if 0 <= x < count:
                    part = piece[:, 128 * k : 128 * k + 128]
                    sums[x] = part if sums[x] is None else sums[x] + part
    size = 3 * rows
    lanes = iota((size, 128), 1)
    result = []
    for x in range(count):
        down, mid, up = (
            sums[x][ez * size : (ez + 1) * size] for ez in range(3)
        )
        down = jnp.where(lanes >= dilate, pltpu.roll(down, dilate, 1), 0.0)
        up = jnp.where(lanes < 128 - dilate, pltpu.roll(up, 128 - dilate, 1), 0.0)
        result.append(mid + down + up)
    return result


def smooth(planes, wy_ref, wz_ref):
    count = len(planes) - 8
    sums = []
    for x in range(count):
        v = planes[x : x + 9]
        sums.append(
            (v[0] + v[8])
            + 2.0 * (v[1] + v[7])
            + 3.0 * (v[2] + v[6])
            + 4.0 * (v[3] + v[5])
            + 5.0 * v[4]
        )
    stacked = jnp.concatenate(split3(jnp.concatenate(sums, axis=1)), axis=0).astype(BF16)
    cols = jnp.dot(wy_ref[...], stacked, preferred_element_type=F32)
    cols = jnp.concatenate([cols[:, x * 128 : (x + 1) * 128] for x in range(count)], axis=0)
    pair = jnp.concatenate(split2(cols), axis=1).astype(BF16)
    return jnp.dot(pair, wz_ref[...], preferred_element_type=F32)


def inner_and_ring(row):
    ring = jnp.where(row == 16, -1, jnp.where(row == 17, 16, -5000))
    return jnp.where(row < 16, row, ring)


def halo_planes(dx, width):
    if dx == 0:
        return 0, width, 4
    many = min(width - 4 * (abs(dx) - 1), 4)
    if dx > 0:
        return 4 - many, width - 4 * dx + 4 - many, many
    return 0, width - 4 * dx, many


def halo_rows(dy, width):
    if dy == 0:
        return 0, 0, 16
    return (16 - width, 16, width) if dy > 0 else (0, 16 + width, width)


def edge_weight(place, extent):
    def missing(n):
        n = jnp.maximum(n, 0)
        return lax.shift_right_logical(n * (n + 1), 1)

    weight = 25 - missing(4 - place) - missing(5 + place - extent)
    return jnp.maximum(weight, 1).astype(F32)


def pair_sum(value, axis, size):
    index = iota(value.shape, axis)
    even = lax.rem(index, 2) == 0
    return value + jnp.where(
        even, pltpu.roll(value, size - 1, axis), pltpu.roll(value, 1, axis)
    )


def kernel(
    slabs,
    groups,
    cap,
    density,
    solid,
    load,
    start,
    stencil,
    owner,
    disp_ref,
    owned_ref,
    st_ref,
    owner_v,
    dens_win,
    sens_win,
    f0,
    coarse,
    load_win,
    solid_win,
    packed,
    mat0,
    mat1,
    mat2,
    wy0_ref,
    wy1_ref,
    wz_ref,
    pick_ref,
    local_sem,
    send_sem,
    recv_sem,
    far_send,
    far_recv,
    give_sem,
    take_sem,
    token_sem,
):
    p = lax.axis_index("slab")
    s = lax.axis_index("blk")

    def neighbour(dx, dy):
        return (lax.rem(p + dx + slabs, slabs), lax.rem(s + dy + groups, groups))

    inner = (p > 1) & (p < slabs - 2) & (s > 0) & (s < groups - 1)

    def each(pairs, act, receive=False):
        pairs = [((-dx, -dy) if receive else (dx, dy), entry) for (dx, dy), entry in pairs]

        @pl.when(inner)
        def _():
            for _, entry in pairs:
                act(entry)

        @pl.when(jnp.logical_not(inner))
        def _():
            for dx, dy in FAR + DIRS:
                group = [entry for where, entry in pairs if where == (dx, dy)]
                if group:
                    inside = (p + dx >= 0) & (p + dx < slabs) & (s + dy >= 0) & (s + dy < groups)

                    @pl.when(inside)
                    def _(group=group):
                        for entry in group:
                            act(entry)

    locals_ = [
        pltpu.make_async_copy(stencil, st_ref, local_sem.at[0]),
        pltpu.make_async_copy(owner, owner_v, local_sem.at[1]),
        pltpu.make_async_copy(start, f0.at[:, 2:6, 0:16], local_sem.at[2]),
        pltpu.make_async_copy(density, dens_win.at[5:9, 0:16], local_sem.at[3]),
        pltpu.make_async_copy(load, load_win.at[:, 1:5, 0:16], local_sem.at[4]),
        pltpu.make_async_copy(solid, solid_win.at[1:5, 0:16], local_sem.at[5]),
    ]
    f0[:, :, 16:24] = jnp.zeros((3, 8, 8, 128), F32)
    dens_win[:, 24:32] = jnp.zeros((14, 8, 128), F32)
    load_win[:, :, 16:24] = jnp.zeros((3, 6, 8, 128), F32)
    solid_win[:, 16:24] = jnp.zeros((6, 8, 128), jnp.int32)

    @pl.when(jnp.logical_not(inner))
    def _():
        f0[...] = jnp.zeros_like(f0)
        dens_win[...] = jnp.zeros_like(dens_win)
        load_win[...] = jnp.zeros_like(load_win)
        solid_win[...] = jnp.zeros_like(solid_win)
        sens_win[...] = jnp.zeros_like(sens_win)
        coarse[...] = jnp.ones_like(coarse)

    barrier = pltpu.get_barrier_semaphore()

    def greet(partner):
        pl.semaphore_signal(barrier, inc=1, device_id=partner, device_id_type=MESH)

    each([((dx, dy), neighbour(dx, dy)) for dx, dy in FAR + DIRS if dx != 0], greet)
    for d in (1, groups - 1):
        greet((p, lax.rem(s + d, groups)))
    for copy in locals_:
        copy.start()

    def count(flag):
        return jnp.where(flag, jnp.int32(1), jnp.int32(0))

    slabs_near = count(p > 0) + count(p < slabs - 1) + count(p > 1) + count(p < slabs - 2)
    pl.semaphore_wait(
        barrier, 2 + slabs_near * (1 + count(s > 0) + count(s < groups - 1))
    )

    started = []

    def window(src, dst, width, lead, base=0):
        def make(dx, dy):
            sx, tx, nx = halo_planes(dx, width)
            sy, ty, ny = halo_rows(dy, width)
            here = (pl.ds(base + sx, nx), pl.ds(sy, ny))
            there = (pl.ds(tx, nx), pl.ds(ty, ny))
            if lead:
                here, there = (slice(None), *here), (slice(None), *there)
            return src.at[here], dst.at[there]

        return make

    def coarse_window(fields):
        def make(dx, dy):
            sy, ty, ny = halo_rows(dy, 4)
            return (
                coarse.at[fields, 1, pl.ds(sy, ny)],
                coarse.at[fields, 1 - dx, pl.ds(ty, ny)],
            )

        return make

    def exchange(rows, far=None):
        copies = []
        by_row = {row: [] for row, _ in rows}

        def add(src, dst, dx, dy, sems):
            copy = pltpu.make_async_remote_copy(
                src_ref=src,
                dst_ref=dst,
                send_sem=sems[0],
                recv_sem=sems[1],
                device_id=neighbour(dx, dy),
                device_id_type=MESH,
            )
            copies.append(((dx, dy), copy))
            return copies[-1]

        for i, (dx, dy) in enumerate(FAR if far is not None else ()):
            add(*far(dx, dy), dx, dy, (far_send.at[i], far_recv.at[i]))
        near = list(enumerate(DIRS))
        order = [(where, entry) for where in near[:6] for entry in rows]
        order += [(where, entry) for entry in rows for where in near[6:]]
        for (i, (dx, dy)), (row, make) in order:
            sems = (send_sem.at[row, i], recv_sem.at[row, i])
            by_row[row].append(add(*make(dx, dy), dx, dy, sems))
        each(copies, lambda copy: copy.start())
        started.extend(copies)
        return by_row, copies[: len(FAR)]

    def arrive(copies):
        each(copies[::-1], lambda copy: copy.wait_recv(), receive=True)

    def tell(stage):
        reach = 2**stage
        if 2 * reach < groups:
            for d in (reach, groups - reach):
                pl.semaphore_signal(
                    token_sem.at[stage],
                    inc=1,
                    device_id=(p, lax.rem(s + d, groups)),
                    device_id_type=MESH,
                )

    def hear(stage):
        if 2 * 2**stage < groups:
            pl.semaphore_wait(token_sem.at[stage], 2)

    far_dens = window(density, dens_win, 5, False)
    inputs, far_in = exchange(
        [
            (1, window(density, dens_win, 5, False)),
            (3, window(solid, solid_win, 1, False)),
            (0, window(start, f0, 2, True)),
            (2, window(load, load_win, 1, True)),
        ],
        far_dens,
    )
    tell(0)

    flags = (s > 0, s < groups - 1)

    def switch(flag):
        return jnp.where(flag, 1.0, 0.0).astype(F32)

    mask_low, mask_high = switch(p > 0), switch(p < slabs - 1)
    locals_[0].wait()
    relax = [OMEGA / jnp.full((8, 128), st_ref[a, a, 13], F32)[0:1, :] for a in range(3)]
    tall = [-relax[a][:, 0:1] for a in range(3)]
    for ex in range(3):
        mat0[ex] = band_matrix(st_ref, ex, inner_and_ring, 24, 2, 1, flags, tall, 1.0)
    for ex in range(3):
        mat1[ex] = band_matrix(st_ref, ex, lambda r: r, 16, 1, 1, flags, None, 0.0)
    for ex in range(3):
        mat2[ex] = band_matrix(st_ref, ex, inner_and_ring, 24, 4, 2, flags, tall, 2.0)

    def triangle(distance):
        return jnp.maximum(5 - jnp.abs(distance), 0).astype(F32).astype(BF16)

    wy0_pos = band_position(lane_mod(iota((24, 96), 1), 32, 2), 5, *flags)
    wy0_ref[...] = triangle(wy0_pos - inner_and_ring(iota((24, 96), 0)))
    wy1_pos = band_position(lane_mod(iota((16, 72), 1), 24, 2), 4, *flags)
    wy1_ref[...] = triangle(wy1_pos - iota((16, 72), 0))
    wz_ref[...] = triangle(lane_mod(iota((256, 128), 0), 128, 1) - iota((256, 128), 1))
    row_y = inner_and_ring(iota((24, 128), 0))
    weight_yz = edge_weight(s * 16 + row_y, 16 * groups) * edge_weight(iota((24, 128), 1), 128)
    inv_weight = []
    for j in range(6):
        weight_x = edge_weight(jnp.full((24, 128), p * 4 + (j - 1), jnp.int32), 4 * slabs)
        inv_weight.append(1.0 / (weight_yz * weight_x))

    locals_[1].wait()
    names = owner_v[...].astype(F32)
    down, across = iota((64, 64), 0), iota((64, 64), 1)
    names_col = jnp.sum(jnp.where(down == across, names, 0.0), axis=1, keepdims=True)
    earlier = (names_col == names) & (across < down)
    rank = jnp.sum(jnp.where(earlier, 1.0, 0.0), axis=1, keepdims=True)
    code_col = names_col * 16.0 + rank
    spread = iota((64, 192), 0) == lane_mod(iota((64, 192), 1), 64, 2)
    code_row = jnp.sum(jnp.where(spread, code_col, 0.0), axis=0, keepdims=True)
    slot = iota((16 * groups, 192), 0).astype(F32)
    pick_ref[...] = jnp.where(slot == code_row, 1.0, 0.0).astype(BF16)

    for copy in locals_[2:6]:
        copy.wait()
    arrive(far_in + inputs[1] + inputs[3])

    hfield = smooth([dens_win[j] for j in range(14)], wy0_ref, wz_ref)
    young, xphys = [], []
    for j in range(6):
        xphys.append(hfield[24 * j : 24 * j + 24] * inv_weight[j])
        solid_f = solid_win[j].astype(F32)
        young.append(EMIN + solid_f * (xphys[j] * xphys[j] * xphys[j]))
    lanes16 = iota((16, 128), 1)
    even_lane = lax.rem(lanes16, 2) == 0

    def coarsen(quarter):
        halves = [
            pair_sum(pair_sum(quarter[2 * i] + quarter[2 * i + 1], 1, 128), 0, 16) * 0.125
            for i in range(2)
        ]
        return jnp.where(even_lane, halves[0], halves[1])

    coarse[3, 1, 0:16] = coarsen([young[1 + x][0:16] for x in range(4)])
    young_in = exchange([(4, coarse_window(pl.ds(3, 1)))])[0][4]
    arrive(inputs[0])
    relaxed = stencil_apply([f0[:, j].reshape(72, 128) for j in range(8)], mat0, 24, 1)
    arrive(inputs[2])
    hear(0)
    tell(1)
    first = []
    for j in range(6):
        inv_young = 1.0 / young[j]
        push = jnp.concatenate(
            [relax[a] * (load_win[a, j] * inv_young) for a in range(3)], axis=0
        )
        first.append(relaxed[j] + push)

    def ends_masked(fields):
        return [fields[0] * mask_low, *fields[1:5], fields[5] * mask_high]

    s_first = stencil_apply(ends_masked(first), mat1, 16, 1)
    for a in range(3):
        coarse[a, 1, 0:16] = coarsen(
            [
                load_win[a, 1 + x, 0:16] - young[1 + x][0:16] * s_first[x][16 * a : 16 * a + 16]
                for x in range(4)
            ]
        )
    coarse_in = exchange([(5, coarse_window(pl.ds(0, 3)))])[0][5]
    sens_scale, out_scale = [], []
    for x in range(4):
        dens = dens_win[5 + x, 0:16]
        solid_f = solid_win[1 + x, 0:16].astype(F32)
        sens_scale.append((-3.0 * dens) * (xphys[1 + x][0:16] * xphys[1 + x][0:16]) * solid_f)
        out_scale.append(inv_weight[1 + x][0:16] / dens)
    arrive(young_in)
    arrive(coarse_in)
    hear(1)
    tell(2)

    even72 = lax.rem(iota((24, 128), 1), 2) == 0
    corr_planes = []
    for plane in range(3):
        inv_cy = 1.0 / coarse[3, plane]
        both = [relax[a] * (coarse[a, plane] * inv_cy) for a in range(3)]
        if plane == 0:
            both = [v * mask_low for v in both]
        if plane == 2:
            both = [v * mask_high for v in both]
        lower = [jnp.where(even72, v, pltpu.roll(v, 1, 1)) for v in both]
        upper = [jnp.where(even72, pltpu.roll(v, 127, 1), v) for v in both]
        corr_planes.append(jnp.concatenate(lower, axis=0))
        corr_planes.append(jnp.concatenate(upper, axis=0))
    corr = stencil_apply(corr_planes, mat2, 24, 2)

    disp = [first[j] + corr[c] for j, c in enumerate((0, 1, 1, 2, 2, 3))]
    corr_fine = [corr[c] for c in (0, 1, 1, 2, 2, 3)]
    s_corr = stencil_apply(ends_masked(corr_fine), mat1, 16, 1)
    s_disp = [s_first[x] + s_corr[x] for x in range(4)]
    for x in range(4):
        energy = None
        for a in range(3):
            term = disp[1 + x][24 * a : 24 * a + 16] * s_disp[x][16 * a : 16 * a + 16]
            energy = term if energy is None else energy + term
        sens_win[4 + x, 0:16] = sens_scale[x] * energy
    sens_in = exchange([(6, window(sens_win, sens_win, 4, False, 4))])[0][6]
    for x in range(4):
        for a in range(3):
            disp_ref[a, x] = disp[1 + x][24 * a : 24 * a + 16]
    arrive(sens_in)
    hear(2)
    filtered = smooth([sens_win[j] for j in range(12)], wy1_ref, wz_ref) * jnp.concatenate(out_scale, axis=0)

    three = jnp.concatenate(split3(filtered), axis=0).astype(BF16)
    rows = jnp.dot(pick_ref[...], three, preferred_element_type=F32)
    for j in range(groups):
        packed[j] = rows[16 * j : 16 * j + cap]
    gives = []
    for d in HANDOUT:
        if d >= groups:
            continue
        target = lax.rem(s + d, groups)
        gives.append(
            pltpu.make_async_remote_copy(
                src_ref=packed.at[target],
                dst_ref=owned_ref.at[:, s],
                send_sem=give_sem.at[d],
                recv_sem=take_sem.at[d],
                device_id=(p, target),
                device_id_type=MESH,
            )
        )
        gives[-1].start()
    own = pltpu.make_async_copy(packed.at[s], owned_ref.at[:, s], local_sem.at[6])
    own.start()
    own.wait()
    each(started, lambda copy: copy.wait_send())
    for copy in gives:
        copy.wait_send()
    for copy in gives[::-1]:
        copy.wait_recv()


def hand_out(disp_in, owned_in, disp_out, owned_out, sems):
    copies = [
        pltpu.make_async_copy(disp_in, disp_out, sems.at[0]),
        pltpu.make_async_copy(owned_in, owned_out, sems.at[1]),
    ]
    for copy in copies:
        copy.start()
    for copy in copies:
        copy.wait()


def on_device(density, solid, load, start, stencil, owner):
    slabs, groups = lax.axis_size("slab"), lax.axis_size("blk")
    cap = CAP
    hbm = pl.BlockSpec(memory_space=pltpu.HBM)
    vmem = pl.BlockSpec(memory_space=pltpu.VMEM)
    operands = (
        density,
        solid,
        load,
        start,
        stencil.transpose(1, 2, 0),
        owner.reshape(1, 64),
    )
    disp, owned = pl.pallas_call(
        functools.partial(kernel, slabs, groups, cap),
        out_shape=(
            pltpu.VMEM(load.shape, F32),
            pltpu.VMEM((cap, groups, 128), F32),
        ),
        in_specs=[hbm] * 6,
        out_specs=(vmem, vmem),
        scratch_shapes=[
            pltpu.SMEM((3, 3, 27), F32),
            pltpu.VMEM((1, 64), jnp.int32),
            pltpu.VMEM((14, 32, 128), F32),
            pltpu.VMEM((12, 24, 128), F32),
            pltpu.VMEM((3, 8, 24, 128), F32),
            pltpu.VMEM((4, 3, 24, 128), F32),
            pltpu.VMEM((3, 6, 24, 128), F32),
            pltpu.VMEM((6, 24, 128), jnp.int32),
            pltpu.VMEM((groups, cap, 128), F32),
            pltpu.VMEM((3, 216, 216), BF16),
            pltpu.VMEM((3, 144, 216), BF16),
            pltpu.VMEM((3, 216, 216), BF16),
            pltpu.VMEM((24, 96), BF16),
            pltpu.VMEM((16, 72), BF16),
            pltpu.VMEM((256, 128), BF16),
            pltpu.VMEM((16 * groups, 192), BF16),
            pltpu.SemaphoreType.DMA((7,)),
            pltpu.SemaphoreType.DMA((7, 8)),
            pltpu.SemaphoreType.DMA((7, 8)),
            pltpu.SemaphoreType.DMA((6,)),
            pltpu.SemaphoreType.DMA((6,)),
            pltpu.SemaphoreType.DMA((groups,)),
            pltpu.SemaphoreType.DMA((groups,)),
            pltpu.SemaphoreType.REGULAR((3,)),
        ],
        compiler_params=pltpu.CompilerParams(
            collective_id=0, has_side_effects=True, vmem_limit_bytes=24 * 1024 * 1024
        ),
    )(*(pltpu.with_memory_space_constraint(x, pltpu.HBM) for x in operands))
    disp, owned = pl.pallas_call(
        hand_out,
        out_shape=(jax.ShapeDtypeStruct(disp.shape, F32), jax.ShapeDtypeStruct(owned.shape, F32)),
        in_specs=[vmem, vmem],
        out_specs=(hbm, hbm),
        scratch_shapes=[pltpu.SemaphoreType.DMA((2,))],
        compiler_params=pltpu.CompilerParams(vmem_limit_bytes=8 * 1024 * 1024),
    )(*(pltpu.with_memory_space_constraint(x, pltpu.VMEM) for x in (disp, owned)))
    return disp, owned.transpose(1, 0, 2)[None, None]


def solution(mesh):
    placed = (
        P("slab", "blk", None),
        P("slab", "blk", None),
        P(None, "slab", "blk", None),
        P(None, "slab", "blk", None),
        P(),
        P("slab", "blk", None, None),
    )
    return jax.shard_map(
        on_device,
        mesh=mesh,
        in_specs=placed,
        out_specs=(P(None, "slab", "blk", None), P("slab", "blk", None, None, None)),
        check_vma=False,
    )
```
